128 devices in a mesh: row: 16 (over x, z), col: 8 (over y, core).
Axes of the slice: x: 4, y: 4, z: 4, core: 2. Of those that a mesh axis runs over, the one named last changes fastest.
Arguments:
- far_left: bfloat16 [16, 8, 128, 128, 256], P('row', 'col'), may hold values from -6.92749e-05 to 6.92749e-05
- far_right: bfloat16 [16, 8, 128, 128, 256], P('row', 'col'), may hold values from -0.47 to 0.47
- far_rank: int32 [16, 8, 128], P('row', 'col'), may hold values from 8 to 128, as said below
- near_tiles: bfloat16 [128, 3, 256, 256], P(('row', 'col')), may hold values from -0.0004108677 to 0.0004108677
- near_cols: int32 [128, 3], P(('row', 'col')), may hold values from 0 to 15, as said below
- data: float32 [16, 8, 256, 128], P('row', 'col'), may hold values from -40 to 40
- reg_weight: float32 [128], replicated, may hold values from 0.05 to 0.5
Outputs:
- solution: float32 [8, 16, 256, 128], P('col', 'row')
- misfit: float32 [16, 8, 256, 128], P('row', 'col')
- regularized: float32 [8, 16, 256, 128], P('col', 'row')
The draws below stay inside these ranges and needn't reach their ends.
Inputs may be any that keep to these rules, and one draw needn't show every extreme that they name: `far_rank`: each leaf's rank is 128 divided by a power of two, at least 1; the first leaf of every device block has rank 128. `near_cols`: the 3 columns of a leaf row I are distinct and lie among five neighbouring leaf columns that contain I % 16 or touch the edge of the column block.
All inputs are finite; a program needn't handle non-finite values.
Results may differ from the reference program's by a relative error of at most 0.0085.
Values may be sent and summed in bfloat16 or wider, within the bound.
No kernel may reach another device: no remote copies, remote signals or barrier semaphores. Data moves between devices by JAX's collectives and lax.ppermute only.
A program may use at most 128 MiB of HBM per device.

```python
import math
import jax
import jax.numpy as jnp
from jax import lax

LEAF = 256
RMAX = 128
BAND = 3
LEAF_ROWS = 8
RHS = 128
ITERS = 2
LEAF_COLS = 16
LEAVES = 128
PIECE = 256
ORDER = 32768
NLEAF = 128
N_ROW = 16
N_COL = 8


def draw_far_rank(key, part):
    key = jax.random.fold_in(key, 11)
    bucket_steps = jax.random.randint(key, (N_ROW, N_COL, LEAVES), 0, 5).astype(jnp.int32)
    largest = jnp.full((N_ROW, N_COL, LEAVES), RMAX, jnp.int32)
    rank_values = jnp.maximum(lax.shift_right_logical(largest, bucket_steps), 1)
    return rank_values.at[:, :, 0].set(RMAX).astype(jnp.int32)


def draw_near_cols(key, part):
    key = jax.random.fold_in(key, 12)
    row_ids = jnp.arange(NLEAF, dtype=jnp.int32)
    diagonal = row_ids % LEAF_COLS
    window_low = jnp.clip(diagonal - 2, 0, LEAF_COLS - 5)
    scores = jax.random.randint(key, (NLEAF, 5), 0, 1 << 20).astype(jnp.int32) * 8 + jnp.arange(5, dtype=jnp.int32)[None, :]
    picked = jnp.argsort(scores, axis=1)[:, :BAND].astype(jnp.int32)
    return (window_low[:, None] + picked).astype(jnp.int32)


def draw_data(key, part):
    key = jax.random.fold_in(key, 13)
    key_base = jax.random.fold_in(key, 1)
    key_scale = jax.random.fold_in(key, 2)
    shape_all = (N_ROW, N_COL, PIECE, RHS)
    base_values = jnp.clip(jax.random.normal(key_base, shape_all, jnp.float32), -4.0, 4.0)
    position = jnp.arange(N_ROW * N_COL * PIECE, dtype=jnp.float32).reshape(N_ROW, N_COL, PIECE, 1) / ORDER
    rising = 1.0 + 2.0 * position
    roughness = 10.0 ** jax.random.uniform(key_scale, (N_ROW, N_COL, PIECE, 1), jnp.float32, -0.5, 0.5)
    return (base_values * rising * roughness).astype(jnp.float32)


def draw_far_left(key, part):
    key = jax.random.fold_in(key, 14)
    key_common = jax.random.fold_in(key, 1)
    key_own = jax.random.fold_in(key, 2)
    root_three = math.sqrt(3.0)
    common = root_three * jax.random.uniform(key_common, (N_ROW, 1, LEAF_ROWS, 1, RMAX, LEAF), jnp.float32, -1.0, 1.0)
    own = root_three * jax.random.uniform(key_own, (N_ROW, N_COL, LEAF_ROWS, LEAF_COLS, RMAX, LEAF), jnp.float32, -1.0, 1.0)
    values = (common + 0.3 * own) * (1.0 / ORDER)
    return values.reshape(N_ROW, N_COL, LEAVES, RMAX, LEAF).astype(jnp.bfloat16)


def draw_far_right(key, part):
    key = jax.random.fold_in(key, 15)
    key_freq = jax.random.fold_in(key, 1)
    key_phase = jax.random.fold_in(key, 2)
    key_noise = jax.random.fold_in(key, 3)
    freq = jax.random.randint(key_freq, (RMAX, 1), 1, ORDER // (2 * LEAF) + 1).astype(jnp.int32)
    phase = jax.random.uniform(key_phase, (RMAX, 1), jnp.float32, -math.pi, math.pi)
    column = jnp.arange(ORDER, dtype=jnp.int32)[None, :]
    turns = (freq * column % ORDER).astype(jnp.float32) / ORDER
    wave = jnp.cos(2.0 * math.pi * turns + phase)
    wave = wave.reshape(RMAX, N_COL, LEAF_COLS, LEAF).transpose(1, 2, 0, 3)
    within = (jnp.arange(LEAF, dtype=jnp.float32) + 0.5) / LEAF
    envelope = 1.0 + 0.7 * jnp.cos(2.0 * math.pi * within)
    decay = 1.0 / (1.0 + 16.0 * jnp.arange(RMAX, dtype=jnp.float32) / RMAX)
    noise = jax.random.uniform(key_noise, (N_ROW, N_COL, LEAF_ROWS, LEAF_COLS, RMAX, LEAF), jnp.float32, -1.0, 1.0)
    values = wave[None, :, None, :, :, :] + 0.08 * noise
    values = 0.25 * values * decay[:, None] * envelope[None, :]
    return values.reshape(N_ROW, N_COL, LEAVES, RMAX, LEAF).astype(jnp.bfloat16)


def draw_near_tiles(key, part):
    key = jax.random.fold_in(key, 16)
    key_spread = jax.random.fold_in(key, 1)
    key_phase = jax.random.fold_in(key, 2)
    key_noise = jax.random.fold_in(key, 3)
    spread = jax.random.uniform(key_spread, (NLEAF, BAND, LEAF, 1), jnp.float32, 0.0, 4.0)
    phase = jax.random.uniform(key_phase, (NLEAF, BAND, LEAF, 1), jnp.float32, -math.pi, math.pi)
    within = ((jnp.arange(LEAF, dtype=jnp.float32) + 0.5) / LEAF)[None, None, None, :]
    profile = jnp.sin(math.pi * within) * jnp.cos(math.pi * spread * within + phase)
    noise = jax.random.uniform(key_noise, (NLEAF, BAND, LEAF, LEAF), jnp.float32, -1.0, 1.0)
    scale = 1.12 / math.sqrt(LEAF * ORDER)
    return (scale * (profile + 0.045 * noise)).astype(jnp.bfloat16)


def setup_inputs(seed: int = 0) -> dict:
    arg_keys = jax.random.split(jax.random.key(seed), 8)
    return {
        "far_left": draw_far_left(jax.random.fold_in(arg_keys[7], 71), 0),
        "far_right": draw_far_right(jax.random.fold_in(arg_keys[7], 71), 0),
        "far_rank": draw_far_rank(jax.random.fold_in(arg_keys[7], 71), 0),
        "near_tiles": draw_near_tiles(jax.random.fold_in(arg_keys[7], 71), 0),
        "near_cols": draw_near_cols(jax.random.fold_in(arg_keys[7], 71), 0),
        "data": draw_data(jax.random.fold_in(arg_keys[7], 71), 0),
        "reg_weight": jnp.clip(jnp.exp(jax.random.uniform(arg_keys[6], (RHS,), jnp.float32, math.log(0.05), math.log(0.5))), 0.05, 0.5),
    }


def round_trip(values):
    return lax.optimization_barrier(values.astype(jnp.bfloat16)).astype(jnp.float32)


def rank_masks(far_rank):
    live_slots = lax.broadcasted_iota(jnp.int32, far_rank.shape + (RMAX,), far_rank.ndim) < far_rank[..., None]
    return live_slots.astype(jnp.float32)


def near_columns(near_cols):
    row_ids = jnp.arange(NLEAF, dtype=jnp.int32)
    return (row_ids // LEAF_COLS)[:, None] * LEAF_COLS + near_cols


def forward(far_left, far_right, masks, near_tiles, near_cols, block_in):
    widened = block_in.astype(jnp.float32)

    def row_product(position):
        left_rows = lax.dynamic_index_in_dim(far_left, position, 0, False).astype(jnp.float32)
        left_rows = left_rows.reshape(N_COL, LEAF_ROWS, LEAF_COLS, RMAX, LEAF)
        right_rows = lax.dynamic_index_in_dim(far_right, position, 0, False).astype(jnp.float32)
        right_rows = right_rows.reshape(N_COL, LEAF_ROWS, LEAF_COLS, RMAX, LEAF)
        mask_rows = lax.dynamic_index_in_dim(masks, position, 0, False).reshape(N_COL, LEAF_ROWS, LEAF_COLS, RMAX, 1)
        coefficient = jnp.einsum("cijkq,cjqn->cijkn", right_rows, widened) * mask_rows
        coefficient = round_trip(coefficient)
        return jnp.einsum("cijkp,cijkn->ipn", left_rows, coefficient)

    result = lax.map(row_product, jnp.arange(N_ROW, dtype=jnp.int32))
    flattened = widened.reshape(N_COL * LEAF_COLS, LEAF, RHS)
    chosen = flattened[near_columns(near_cols)]
    near_term = jnp.einsum("ebpq,ebqn->epn", near_tiles.astype(jnp.float32), chosen)
    return result + near_term.reshape(N_ROW, LEAF_ROWS, LEAF, RHS)


def adjoint(far_left, far_right, masks, near_tiles, near_cols, block_in):
    widened = block_in.astype(jnp.float32)

    def column_product(position):
        left_cols = lax.dynamic_index_in_dim(far_left, position, 1, False).astype(jnp.float32)
        left_cols = left_cols.reshape(N_ROW, LEAF_ROWS, LEAF_COLS, RMAX, LEAF)
        right_cols = lax.dynamic_index_in_dim(far_right, position, 1, False).astype(jnp.float32)
        right_cols = right_cols.reshape(N_ROW, LEAF_ROWS, LEAF_COLS, RMAX, LEAF)
        mask_cols = lax.dynamic_index_in_dim(masks, position, 1, False).reshape(N_ROW, LEAF_ROWS, LEAF_COLS, RMAX, 1)
        coefficient = jnp.einsum("rijkp,ripn->rijkn", left_cols, widened) * mask_cols
        coefficient = round_trip(coefficient)
        return jnp.einsum("rijkq,rijkn->jqn", right_cols, coefficient)

    result = lax.map(column_product, jnp.arange(N_COL, dtype=jnp.int32))
    term_list = jnp.einsum("ebpq,epn->ebqn", near_tiles.astype(jnp.float32), widened.reshape(NLEAF, LEAF, RHS))
    flattened = jnp.zeros((N_COL * LEAF_COLS, LEAF, RHS), jnp.float32)
    flattened = flattened.at[near_columns(near_cols).reshape(-1)].add(term_list.reshape(-1, LEAF, RHS))
    return result + flattened.reshape(N_COL, LEAF_COLS, LEAF, RHS)


def smoothing(vector):
    flattened = vector.reshape(-1, RHS)
    padded = jnp.pad(flattened, ((1, 1), (0, 0)))
    return (2.0 * flattened - padded[:-2] - padded[2:]).reshape(vector.shape)


def reference(far_left, far_right, far_rank, near_tiles, near_cols, data, reg_weight):
    masks = rank_masks(far_rank)
    residual = data.reshape(N_ROW, LEAF_ROWS, LEAF, RHS)
    solution = jnp.zeros((N_COL, LEAF_COLS, LEAF, RHS), jnp.float32)
    descent = adjoint(far_left, far_right, masks, near_tiles, near_cols, residual.astype(jnp.bfloat16))
    direction = descent
    gradient_sq = jnp.sum(descent * descent, axis=(0, 1, 2))
    for iteration in range(ITERS):
        mapped = forward(far_left, far_right, masks, near_tiles, near_cols, direction.astype(jnp.bfloat16))
        curved = smoothing(direction)
        delta = jnp.sum(mapped * mapped, axis=(0, 1, 2)) + reg_weight * jnp.sum(direction * curved, axis=(0, 1, 2))
        step_size = gradient_sq / delta
        solution = solution + step_size * direction
        residual = residual - step_size * mapped
        if iteration + 1 < ITERS:
            descent = adjoint(far_left, far_right, masks, near_tiles, near_cols, residual.astype(jnp.bfloat16))
            descent = descent - reg_weight * smoothing(solution)
            fresh_norm = jnp.sum(descent * descent, axis=(0, 1, 2))
            direction = descent + (fresh_norm / gradient_sq) * direction
            gradient_sq = fresh_norm
    regularized = smoothing(solution)
    return (solution.reshape(N_COL, N_ROW, PIECE, RHS), residual.reshape(N_ROW, N_COL, PIECE, RHS), regularized.reshape(N_COL, N_ROW, PIECE, RHS))
```

```python
import jax
import jax.numpy as jnp
from jax import lax
from jax.experimental import pallas as pl
from jax.experimental.pallas import tpu as pltpu
from jax.sharding import PartitionSpec as P

F32 = jnp.float32
BF16 = jnp.bfloat16
ROWS = 16
COLS = 8
RANK = 128
RHS = 128
LEAF = 256
BAND = 3
EXTRA = 16
MSG = RHS + EXTRA
ORDER = (1, 3, 2)
FULL = 32000.0
VMEM = pl.BlockSpec(memory_space=pltpu.VMEM)
SMEM = pl.BlockSpec(memory_space=pltpu.SMEM)
HBM = pl.BlockSpec(memory_space=pl.ANY)


def shape(dims, dtype=F32):
    return jax.ShapeDtypeStruct(dims, dtype)


def call(kernel, outs, *args, specs=None, scratch=(), limit=8, flops=0):
    return pl.pallas_call(
        kernel,
        out_shape=outs,
        in_specs=specs or [VMEM] * len(args),
        out_specs=jax.tree.map(lambda _: VMEM, outs),
        scratch_shapes=list(scratch),
        compiler_params=pltpu.CompilerParams(vmem_limit_bytes=limit << 20),
        cost_estimate=pl.CostEstimate(flops=flops, bytes_accessed=1 << 16, transcendentals=0),
    )(*args)


def nt(left, right):
    return lax.dot_general(left, right, (((1,), (1,)), ((), ())), preferred_element_type=F32)


def nn(left, right):
    return jnp.dot(left, right, preferred_element_type=F32)


def row_sum(values):
    folded = values[:, :RHS] + values[:, RHS:]
    return jnp.sum(folded.T, axis=0, keepdims=True)


def as_column(row):
    square = jnp.broadcast_to(row, (RHS, RHS)).T
    return jnp.concatenate([square, square], axis=1)


def split3(row):
    high = row.astype(BF16).astype(F32)
    middle = (row - high).astype(BF16).astype(F32)
    return [high, middle, row - high - middle]


def code_of(largest):
    return jnp.ceil(jnp.log2(jnp.maximum(largest, 1e-30)) * 128.0)


def size_of(code):
    return jnp.exp2(code * (1.0 / 128.0))


def to_int16(values):
    return jnp.round(values).astype(jnp.int32).astype(jnp.int16)


def encode_rows(sums):
    rows = []
    for value in sums:
        code = code_of(jnp.abs(value))
        scaled = value / size_of(code) * FULL
        whole = jnp.round(scaled)
        rows += [code, whole, jnp.round((scaled - whole) * 65000.0)]
    return rows


def decode_rows(extra):
    rows = extra[...].astype(jnp.int32).astype(F32)[:, :RHS]
    sums = []
    for at in (4, 7):
        whole = rows[at + 1 : at + 2] + rows[at + 2 : at + 3] * (1.0 / 65000.0)
        sums.append(size_of(rows[at : at + 1]) * whole * (1.0 / FULL))
    return sums


def encode(out, pieces, sums):
    lane = lax.broadcasted_iota(jnp.int32, (RHS, RHS), 1)
    codes = jnp.zeros((RHS, RHS), F32)
    for m, piece in enumerate(pieces):
        code = code_of(jnp.max(jnp.abs(piece), axis=1, keepdims=True))
        out[m * RHS : (m + 1) * RHS] = to_int16(piece * (FULL / size_of(code)))
        codes = jnp.where(lane == m, code, codes)
    rows = jnp.concatenate([codes.T[:4]] + encode_rows(sums) + [jnp.zeros((EXTRA - 10, RHS), F32)], axis=0)
    out[len(pieces) * RHS :] = to_int16(jnp.concatenate([rows, jnp.zeros_like(rows)], axis=1))


def decode(message, count):
    rows = message[count * RHS :].astype(jnp.int32).astype(F32)[:, :RHS]
    square = jnp.concatenate([rows, jnp.zeros((RHS - EXTRA, RHS), F32)], axis=0).T
    pieces = []
    for m in range(count):
        scale = size_of(square[:, m : m + 1]) * (1.0 / FULL)
        pieces.append(message[m * RHS : (m + 1) * RHS].astype(jnp.int32).astype(F32) * scale)
    return pieces


def two_rows(rows):
    return jnp.concatenate([rows[0], rows[1], jnp.zeros((6, RHS), F32)], axis=0)


def live_pair(live, leaf_a, leaf_b):
    return jnp.concatenate([live[pl.ds(leaf_a, 1), :], live[pl.ds(leaf_b, 1), :]], axis=1)


def first_message(data, extra, out):
    out[:RHS] = data[...].T.astype(BF16)
    out[RHS:] = extra[...]


M_ROW, M_HALO, M_OWNER, M_AT, M_ODD, M_COL = 16, 24, 26, 27, 28, 29


def slot_of(meta, column):
    apart = column ^ meta[M_AT]
    swapped = (apart % 4) * 4 + apart // 4
    return jnp.where(meta[M_ODD] == 1, swapped, apart)


def tile_at(tiles, s, k):
    return tiles[s % 4][BAND * (s // 4) + k]


def data_pieces(group, other):
    return [a[:RHS] for a in group] + [other[MSG * m : MSG * m + RHS] for m in range(4)]


def data_extras(group, other):
    return [a[RHS:] for a in group] + [other[MSG * m + RHS : MSG * (m + 1)] for m in range(4)]


def add_near_terms(meta, cols, pieces, tiles, near):
    near[...] = jnp.zeros_like(near)

    @pl.when(meta[M_OWNER] == 1)
    def _():
        for s in range(COLS):
            for k in range(BAND):
                slot = slot_of(meta, cols[s, k])
                near[slot] += nn(pieces[s], tile_at(tiles, s, k))


def far_pair(meta, live, left, right, pieces, slot):
    ja, jb = meta[slot], meta[slot + 1]
    coef_a, coef_b, right_a, right_b = [], [], [], []
    for s in range(COLS):
        base = meta[M_ROW + s] * ROWS
        pair = jnp.concatenate([left[base + ja], left[base + jb]], axis=0)
        coef = (nt(pieces[s], pair) * live_pair(live, base + ja, base + jb)).astype(BF16)
        coef_a.append(coef[:, :RANK])
        coef_b.append(coef[:, RANK:])
        right_a.append(right[base + ja])
        right_b.append(right[base + jb])
    part_a = nn(jnp.concatenate(coef_a, axis=1), jnp.concatenate(right_a, axis=0))
    part_b = nn(jnp.concatenate(coef_b, axis=1), jnp.concatenate(right_b, axis=0))
    return part_a, part_b


def far_group(meta, live, left, right, pieces, m2):
    first = far_pair(meta, live, left, right, pieces, 4 * m2)
    return first + far_pair(meta, live, left, right, pieces, 4 * m2 + 2)


def far_only_kernel(meta, live, left, right, a0, a1, a2, a3, b, far, cols):
    pieces = data_pieces((a0, a1, a2, a3), b)
    rows = [extra.astype(F32)[:1, :RHS] for extra in data_extras((a0, a1, a2, a3), b)]
    cols[...] = jnp.concatenate(rows, axis=0).astype(jnp.int32)
    for m2 in range(4):
        for m1, part in enumerate(far_group(meta, live, left, right, pieces, m2)):
            far[4 * m2 + m1] = part


def near_encode_kernel(meta, cols, far, a0, a1, a2, a3, b, t0, t1, t2, t3, g1, g3, g2, own_out, near):
    add_near_terms(meta, cols, data_pieces((a0, a1, a2, a3), b), (t0, t1, t2, t3), near)
    zero = jnp.zeros((1, RHS), F32)
    for m2, out in ((1, g1), (3, g3), (2, g2)):
        encode(out, [far[4 * m2 + m] + near[4 * m2 + m] for m in range(4)], [zero, zero])
    for m in range(4):
        own_out[m * RHS : (m + 1) * RHS] = far[m] + near[m]


def adjoint_first_kernel(
    meta, cols, reg, live, left, right, a0, a1, a2, a3, b, t0, t1, t2, t3, g1, g3, g2, near, sums_out, rims_out, first, last
):
    pieces = data_pieces((a0, a1, a2, a3), b)
    sums = [jnp.zeros((1, RHS), F32)] * 2
    for s, extra in enumerate(data_extras((a0, a1, a2, a3), b)):
        terms = extra.astype(F32)[:, :RHS]
        sums = [sums[0] + (terms[0:1] + terms[1:2] + terms[2:3]), sums[1] + (terms[3:4] + terms[4:5] + terms[5:6])]
        column = meta[M_ROW + s]
        first[pl.ds(column, 1), :] = terms[6:7]
        last[pl.ds(column, 1), :] = terms[7:8]
    at, column = meta[M_AT], meta[M_COL]
    cross = jnp.sum(last[0 : COLS - 1] * first[1:COLS], axis=0, keepdims=True)
    sums[1] += jnp.where(at == 0, -2.0 * reg[...] * cross, 0.0)
    before = last[pl.ds(jnp.maximum(column - 1, 0), 1), :]
    after = first[pl.ds(jnp.minimum(column + 1, COLS - 1), 1), :]
    rims_out[...] = two_rows(
        [
            jnp.where(column > 0, before, 0.0),
            jnp.where(column < COLS - 1, after, 0.0),
        ]
    )
    sums_out[...] = two_rows(sums)
    add_near_terms(meta, cols, pieces, (t0, t1, t2, t3), near)
    for m2, out in ((1, g1), (3, g3), (2, g2)):
        parts = far_group(meta, live, left, right, pieces, m2)
        encode(out, [part + near[4 * m2 + m] for m, part in enumerate(parts)], sums)


def adjoint_second_kernel(meta, live, left, right, a0, a1, a2, a3, b, near, own_out):
    pieces = data_pieces((a0, a1, a2, a3), b)
    for m, part in enumerate(far_group(meta, live, left, right, pieces, 0)):
        own_out[m * RHS : (m + 1) * RHS] = part + near[m]


def coefficient_pair(meta, live, right, held, s, slots):
    base_a, base_b = meta[M_ROW + s] * ROWS, meta[M_ROW + s + 1] * ROWS
    coef_a, coef_b = [], []
    for slot in slots:
        j = meta[slot]
        pair = jnp.concatenate([right[base_a + j], right[base_b + j]], axis=0)
        coef = (nt(held(slot), pair) * live_pair(live, base_a + j, base_b + j)).astype(BF16)
        coef_a.append(coef[:, :RANK])
        coef_b.append(coef[:, RANK:])
    return jnp.concatenate(coef_a, axis=1), jnp.concatenate(coef_b, axis=1)


def piece_of(arrays):
    def held(slot):
        return arrays[slot // 4][(slot % 4) * RHS : (slot % 4 + 1) * RHS]

    return held


def coefficient_kernel(meta, live, right, a, coef):
    for s in (4, 6, 0, 2):
        coef[s], coef[s + 1] = coefficient_pair(meta, live, right, piece_of((a,)), s, range(4))


def forward_rows(meta, cols, live, left, right, coef, arrays, tiles, out, near, held, start):
    piece = piece_of(arrays)
    for slot in range(ROWS):
        held[slot] = piece(slot)
    near[...] = jnp.zeros_like(near)

    @pl.when(meta[M_OWNER] == 1)
    def _():
        for m in range(4):
            for k in range(BAND):
                slot = slot_of(meta, cols[start + m, k])
                near[m] += nt(held[slot], tile_at(tiles, start + m, k))

    for m in (0, 2):
        s = start + m
        more = coefficient_pair(meta, live, right, piece, s, range(4, ROWS))
        for at in range(2):
            base = meta[M_ROW + s + at] * ROWS
            factor = jnp.concatenate([left[base + meta[slot]] for slot in range(ROWS)], axis=0)
            value = nn(jnp.concatenate([coef[s + at], more[at]], axis=1), factor) + near[m + at]
            out[(m + at) * RHS : (m + at + 1) * RHS] = value.astype(out.dtype)


def forward_first_kernel(
    meta, cols, live, left, right, coef, a, b1, b2, b3, t0, t1, t2, t3, out, held, near
):
    forward_rows(
        meta, cols, live, left, right, coef, (a, b1, b2, b3), (t0, t1, t2, t3), out, near, held, 4
    )


def forward_second_kernel(
    meta, cols, live, left, right, coef, a, b1, b2, b3, t0, t1, t2, t3, own, out, curved, edges, held, near
):
    forward_rows(
        meta, cols, live, left, right, coef, (a, b1, b2, b3), (t0, t1, t2, t3), out, near, held, 0
    )
    lane = lax.broadcasted_iota(jnp.int32, (RHS, LEAF), 1)
    for m in range(4):
        rows = slice(m * RHS, (m + 1) * RHS)
        vector, j = own[rows], meta[m]
        before = held[slot_of(meta, (j + ROWS - 1) % ROWS)][:, LEAF - RHS :].astype(F32)[:, RHS - 1 :]
        after = held[slot_of(meta, (j + 1) % ROWS)][:, :RHS].astype(F32)[:, :1]
        before = jnp.where(j == 0, 0.0, before)
        after = jnp.where(j == ROWS - 1, 0.0, after)
        below = jnp.where(lane == 0, before, pltpu.roll(vector, 1, 1))
        above = jnp.where(lane == LEAF - 1, after, pltpu.roll(vector, LEAF - 1, 1))
        curved[rows] = 2.0 * vector - below - above
    first = held[slot_of(meta, 0)][:, :RHS].astype(F32).T[:1]
    last = held[slot_of(meta, ROWS - 1)][:, LEAF - RHS :].astype(F32).T[RHS - 1 :]
    edges[...] = two_rows([first, last])


def without_rims(curved, before, after, j):
    lane = lax.broadcasted_iota(jnp.int32, (RHS, LEAF), 1)
    curved = curved - jnp.where((lane == 0) & (j == 0), before, 0.0)
    return curved - jnp.where((lane == LEAF - 1) & (j == ROWS - 1), after, 0.0)


def row_phase_kernel(own, sums_in, g1, g3, g2, own_out, sums_out, message):
    sums = [sums_in[0:1], sums_in[1:2]]
    totals = [own[m * RHS : (m + 1) * RHS] for m in range(4)]
    for g in (g1, g3, g2):
        sums = [x + y for x, y in zip(sums, decode_rows(g[4 * RHS :]))]
        totals = [x + y for x, y in zip(totals, decode(g, 4))]
    sums_out[...] = two_rows(sums)
    encode(message, totals, sums)
    for m in range(4):
        own_out[m * RHS : (m + 1) * RHS] = totals[m]


def group_totals(own, p1, p3, p2):
    totals = [own[m * RHS : (m + 1) * RHS] for m in range(4)]
    for k, p in ((1, p1), (3, p3), (2, p2)):
        got = decode(p, 4)
        totals = [total + got[k ^ m] for m, total in enumerate(totals)]
    return totals


def descent_kernel(own, p1, p3, p2, full, sent):
    for m, total in enumerate(group_totals(own, p1, p3, p2)):
        full[m * RHS : (m + 1) * RHS] = total
        sent[m * RHS : (m + 1) * RHS] = total.astype(BF16)


def descent2_kernel(meta, reg, first, curved, rims, own, sums_in, p1, p3, p2, full, sent, curved_out, sums_out):
    sums = [sums_in[0:1], sums_in[1:2]]
    for p in (p1, p3, p2):
        sums = [x + y for x, y in zip(sums, decode_rows(p[4 * RHS :]))]
    sums_out[...] = two_rows(sums)
    step, weight = as_column(sums[0] / sums[1]), as_column(reg[...])
    before, after = as_column(rims[0:1]), as_column(rims[1:2])
    for m, total in enumerate(group_totals(own, p1, p3, p2)):
        rows = slice(m * RHS, (m + 1) * RHS)
        whole = without_rims(curved[rows], before, after, meta[m])
        curved_out[rows] = whole
        vector = first[rows] - step * (total + weight * whole)
        full[rows] = vector
        sent[rows] = vector.astype(BF16)


def core_phase_kernel(own, other, own_out, p1, p3, p2):
    for m, out in ((1, p1), (3, p3), (2, p2), (0, own_out)):
        rows = slice(m * RHS, (m + 1) * RHS)
        out[...] = (own[rows] + other[rows].astype(F32)).astype(out.dtype)


def image_kernel(reg, vector, curved, edges, own, p1, p3, p2, full, message):
    total = own[...]
    for p in (p1, p3, p2):
        total += p[...].astype(F32)
    full[...] = total
    value = vector[:RHS]
    message[:RHS] = total.astype(BF16)
    gamma = row_sum(value * value)
    delta = row_sum(total * total) + reg[...] * row_sum(value * curved[:RHS])
    rows = jnp.concatenate(
        split3(gamma) + split3(delta) + [edges[0:2], jnp.zeros((EXTRA - 8, RHS), F32)], axis=0
    )
    message[RHS:] = jnp.concatenate([rows, jnp.zeros_like(rows)], axis=1).astype(BF16)


def image2_kernel(meta, reg, vector, curved, edges, curved_first, first, own, p1, p3, p2, full, sums):
    total = own[...]
    for p in (p1, p3, p2):
        total += p[...].astype(F32)
    full[...] = total
    value = vector[:RHS]
    weight = reg[...]
    sums[...] = jnp.zeros_like(sums)
    sums[0:1] = row_sum(value * value)
    sums[1:2] = row_sum(total * total) + weight * row_sum(value * curved[:RHS])
    sums[2:3] = row_sum(total * first[...]) + weight * row_sum(value * curved_first[:RHS])
    column = meta[M_COL]
    sums[pl.ds(8 + column, 1), :] = jnp.where(meta[M_AT] == 0, edges[0:1], 0.0)
    sums[pl.ds(16 + column, 1), :] = jnp.where(meta[M_AT] == 0, edges[1:2], 0.0)


def final_kernel(meta, reg, sums1, sums2, s1, s2, d1, d2, y1, y2, data, solution_out, misfit_out, curved_out):
    gamma, delta = sums1[0:1], sums1[1:2]
    first, last = sums2[8 : 8 + COLS], sums2[16 : 16 + COLS]
    cross = jnp.sum(last[: COLS - 1] * first[1:], axis=0, keepdims=True)
    fresh, delta_new, delta_mixed = sums2[0:1], sums2[1:2] - 2.0 * reg[...] * cross, sums2[2:3]
    column = meta[M_COL]
    before = sums2[pl.ds(16 + jnp.maximum(column - 1, 0), 1), :]
    after = sums2[pl.ds(8 + jnp.minimum(column + 1, COLS - 1), 1), :]
    rims = [
        jnp.where(column > 0, before, 0.0),
        jnp.where(column < COLS - 1, after, 0.0),
    ]
    beta = fresh / gamma
    delta2 = delta_new + 2.0 * beta * delta_mixed + beta * beta * delta
    step2 = fresh / delta2
    one = as_column(gamma / delta + step2 * beta)
    two = as_column(step2)
    whole = without_rims(d2[:RHS], as_column(rims[0]), as_column(rims[1]), meta[M_AT])
    solution_out[...] = (one * s1[:RHS] + two * s2[:RHS]).T
    curved_out[...] = (one * d1[:RHS] + two * whole).T
    misfit_out[...] = data[...] - (one * y1[...] + two * y2[...]).T


def grid_pairs(move):
    return [(r * COLS + c, to) for r in range(ROWS) for c in range(COLS) for to in [move(r, c)] if to is not None]


def send(value, move):
    return lax.ppermute(value, ("row", "col"), grid_pairs(move))


def near_move(m):
    return lambda r, c: (r ^ (m if c % 2 == 0 else 4 * m)) * COLS + c


def far_move(m):
    return lambda r, c: (r ^ (4 * m if c % 2 == 0 else m)) * COLS + c


def y_move(m):
    return lambda r, c: r * COLS + (c ^ (2 * m))


def core_move(r, c):
    return r * COLS + (c ^ 1)


def tile_core_move(r, c):
    return r * COLS + (c ^ 1) if c % 2 != (r // 2) % 2 else None


def tile_move(m):
    def move(r, c):
        owner = r // 2
        there = c % 2 == owner % 2 and (c // 2) ^ (owner // 2) == m
        return r * COLS + (c ^ (2 * m)) if there else None

    return move


def per_device(far_left, far_right, far_rank, near_tiles, near_cols, data, reg_weight):
    r = lax.axis_index("row")
    c = lax.axis_index("col")
    odd = c % 2
    leaves = far_rank.shape[-1]

    def at_slot(m2, m1):
        return jnp.where(odd == 0, r ^ m1 ^ (4 * m2), r ^ (4 * m1) ^ m2)

    def slot_at(column):
        apart = column ^ r
        return jnp.where(odd == 1, (apart % 4) * 4 + apart // 4, apart)

    meta = jnp.stack(
        [at_slot(s // 4, s % 4) for s in range(ROWS)]
        + [c ^ (2 * (s % 4)) ^ (s // 4) for s in range(COLS)]
        + [slot_at((r + ROWS - 1) % ROWS), slot_at((r + 1) % ROWS)]
        + [(c == r // 2).astype(jnp.int32), r, odd, c]
    ).astype(jnp.int32)
    reg = reg_weight.reshape(1, RHS)
    data = data.reshape(LEAF, RHS)

    cols_row = jnp.pad(near_cols.astype(BF16), ((0, EXTRA - 1), (0, LEAF - BAND)))
    message = call(first_message, shape((MSG, LEAF), BF16), data, cols_row)

    def gather_col_pieces(mine):
        got = {m: send(mine, y_move(m)) for m in ORDER}
        return [mine, got[1], got[2], got[3]]

    group = gather_col_pieces(message)
    tiles, _ = lax.optimization_barrier((near_tiles.reshape(BAND, LEAF, LEAF), message))
    tiles = jnp.concatenate([tiles, send(tiles, tile_core_move)], axis=0)
    tiles, _ = lax.optimization_barrier((tiles, group))
    tiles = [tiles] + [send(tiles, tile_move(m)) for m in (1, 2, 3)]
    left = far_left.reshape(leaves, RANK, LEAF)
    right = far_right.reshape(leaves, RANK, LEAF)
    live = (lax.broadcasted_iota(jnp.int32, (leaves, RANK), 1) < far_rank.reshape(leaves, 1)).astype(F32)
    other = send(jnp.concatenate(group, axis=0), core_move)

    def factors():
        return [live] + [pltpu.with_memory_space_constraint(x, pltpu.VMEM) for x in (left, right)]

    vec, sums_shape = shape((RHS, LEAF)), shape((8, RHS))
    sent_shape = shape((RHS, LEAF), BF16)
    group4, group4_sent = shape((4 * RHS, LEAF)), shape((4 * RHS, LEAF), BF16)
    big = shape((4 * RHS + EXTRA, LEAF), jnp.int16)
    near_shape = shape((ROWS, RHS, LEAF))
    near_scratch = pltpu.VMEM((ROWS, RHS, LEAF), F32)

    def specs(scalars, vectors):
        return [SMEM] * scalars + [VMEM] * vectors

    def sum_over_row(own, sums, parts):
        got = [send(g, far_move(m)) for m, g in zip(ORDER, parts)]
        own, sums, message = call(row_phase_kernel, (group4, sums_shape, big), own, sums, *got)
        return own, sums, [send(message, near_move(m)) for m in ORDER]

    def product(vector, sent):
        got = {m: send(sent, far_move(m)) for m in ORDER}
        pieces = [sent, got[1], got[2], got[3]]
        coef = call(
            coefficient_kernel, shape((COLS, RHS, 4 * RANK), BF16), meta, live, factors()[2], sent,
            specs=specs(1, 3), flops=1 << 28,
        )
        scratch = [pltpu.VMEM((ROWS, RHS, LEAF), BF16), pltpu.VMEM((4, RHS, LEAF), F32)]
        parts = call(
            forward_first_kernel, group4_sent, meta, cols, *factors(), coef, *pieces, *tiles,
            specs=specs(2, 12), scratch=scratch, flops=1 << 30,
        )
        other = send(parts, core_move)
        own, curved, edges = call(
            forward_second_kernel, (group4, group4, sums_shape), meta, cols, *factors(), coef, *pieces, *tiles, vector,
            specs=specs(2, 13), scratch=scratch, flops=1 << 30,
        )
        own, p1, p3, p2 = call(core_phase_kernel, (vec, sent_shape, sent_shape, sent_shape), own, other)
        return curved, edges, [own] + [send(p, y_move(m)) for m, p in zip(ORDER, (p1, p3, p2))]

    far, cols = call(
        far_only_kernel, (near_shape, shape((COLS, RHS), jnp.int32)), meta, *factors(), *group, other,
        specs=specs(1, 8), flops=1 << 31,
    )
    g1, g3, g2, own = call(
        near_encode_kernel, (big, big, big, group4), meta, cols, far, *group, other, *tiles,
        specs=specs(2, 10), scratch=[near_scratch], flops=1 << 29,
    )
    own, _, parts = sum_over_row(own, jnp.zeros((8, RHS), F32), (g1, g3, g2))
    s1, s1_sent = call(descent_kernel, (group4, group4_sent), own, *parts)
    d1, edges, parts = product(s1, s1_sent)
    y1, message = call(image_kernel, (vec, shape((MSG, LEAF), BF16)), reg, s1, d1, edges, *parts)

    group = gather_col_pieces(message)
    other = send(jnp.concatenate(group, axis=0), core_move)
    g1, g3, g2, near, sums, rims = call(
        adjoint_first_kernel, (big, big, big, near_shape, sums_shape, sums_shape),
        meta, cols, reg, *factors(), *group, other, *tiles,
        specs=specs(2, 13), scratch=[pltpu.VMEM((COLS, RHS), F32)] * 2, flops=1 << 30,
    )
    own = call(
        adjoint_second_kernel, group4, meta, *factors(), *group, other, near,
        specs=specs(1, 9), flops=1 << 30,
    )
    own, sums, parts = sum_over_row(own, sums, (g1, g3, g2))
    s2, s2_sent, d1, sums1 = call(
        descent2_kernel, (group4, group4_sent, group4, sums_shape), meta, reg, s1, d1, rims, own, sums, *parts,
        specs=specs(1, 9),
    )
    d2, edges, parts = product(s2, s2_sent)
    y2, sums2 = call(
        image2_kernel, (vec, shape((24, RHS))), meta, reg, s2, d2, edges, d1, y1, *parts, specs=specs(1, 10)
    )
    sums2 = sums2 + send(sums2, core_move)
    for move in (y_move, near_move, far_move):
        got = {m: send(sums2, move(m)) for m in ORDER}
        sums2 = (sums2 + got[1]) + (got[2] + got[3])
    piece = shape((LEAF, RHS))
    solution_out, misfit_out, curved_out = call(
        final_kernel, (piece, piece, piece), meta, reg, sums1, sums2, s1, s2, d1, d2, y1, y2, data, specs=specs(1, 10)
    )
    whole = (1, 1, LEAF, RHS)
    return solution_out.reshape(whole), misfit_out.reshape(whole), curved_out.reshape(whole)


def solution(mesh):
    in_specs = (
        P("row", "col", None, None, None),
        P("row", "col", None, None, None),
        P("row", "col", None),
        P(("row", "col"), None, None, None),
        P(("row", "col"), None),
        P("row", "col", None, None),
        P(),
    )
    out_specs = (
        P("col", "row", None, None),
        P("row", "col", None, None),
        P("col", "row", None, None),
    )
    return jax.shard_map(
        per_device, mesh=mesh, in_specs=in_specs, out_specs=out_specs, check_vma=False
    )
```

```python
import jax
import jax.numpy as jnp
from jax import lax
from jax.experimental import pallas as pl
from jax.experimental.pallas import tpu as pltpu
from jax.sharding import PartitionSpec as P

F32 = jnp.float32
BF16 = jnp.bfloat16
ROWS = 16
COLS = 8
RANK = 128
RHS = 128
LEAF = 256
BAND = 3
EXTRA = 16
MSG = RHS + EXTRA
ORDER = (1, 3, 2)
SUMS = 24
FULL = 32000.0
VMEM = pl.BlockSpec(memory_space=pltpu.VMEM)
SMEM = pl.BlockSpec(memory_space=pltpu.SMEM)
HBM = pl.BlockSpec(memory_space=pl.ANY)


def shape(dims, dtype=F32):
    return jax.ShapeDtypeStruct(dims, dtype)


def call(kernel, outs, *args, specs=None, scratch=(), limit=8, flops=0):
    return pl.pallas_call(
        kernel,
        out_shape=outs,
        in_specs=specs or [VMEM] * len(args),
        out_specs=jax.tree.map(lambda _: VMEM, outs),
        scratch_shapes=list(scratch),
        compiler_params=pltpu.CompilerParams(vmem_limit_bytes=limit << 20),
        cost_estimate=pl.CostEstimate(flops=flops, bytes_accessed=1 << 16, transcendentals=0),
    )(*args)


def nt(left, right):
    return lax.dot_general(left, right, (((1,), (1,)), ((), ())), preferred_element_type=F32)


def nn(left, right):
    return jnp.dot(left, right, preferred_element_type=F32)


def row_sum(values):
    folded = values[:, :RHS] + values[:, RHS:]
    return jnp.sum(folded.T, axis=0, keepdims=True)


def as_column(row):
    square = jnp.broadcast_to(row, (RHS, RHS)).T
    return jnp.concatenate([square, square], axis=1)


def split3(row):
    high = row.astype(BF16).astype(F32)
    middle = (row - high).astype(BF16).astype(F32)
    return [high, middle, row - high - middle]


def code_of(largest):
    return jnp.ceil(jnp.log2(jnp.maximum(largest, 1e-30)) * 128.0)


def size_of(code):
    return jnp.exp2(code * (1.0 / 128.0))


def to_int16(values):
    return jnp.round(values).astype(jnp.int32).astype(jnp.int16)


def encode_rows(sums):
    rows = []
    for value in sums:
        code = code_of(jnp.abs(value))
        scaled = value / size_of(code) * FULL
        whole = jnp.round(scaled)
        rows += [code, whole, jnp.round((scaled - whole) * 65000.0)]
    return rows


def decode_rows(extra):
    rows = extra[...].astype(jnp.int32).astype(F32)[:, :RHS]
    sums = []
    for at in (4, 7):
        whole = rows[at + 1 : at + 2] + rows[at + 2 : at + 3] * (1.0 / 65000.0)
        sums.append(size_of(rows[at : at + 1]) * whole * (1.0 / FULL))
    return sums


def encode(out, pieces, sums):
    lane = lax.broadcasted_iota(jnp.int32, (RHS, RHS), 1)
    codes = jnp.zeros((RHS, RHS), F32)
    for m, piece in enumerate(pieces):
        code = code_of(jnp.max(jnp.abs(piece), axis=1, keepdims=True))
        out[m * RHS : (m + 1) * RHS] = to_int16(piece * (FULL / size_of(code)))
        codes = jnp.where(lane == m, code, codes)
    rows = jnp.concatenate([codes.T[:4]] + encode_rows(sums) + [jnp.zeros((EXTRA - 10, RHS), F32)], axis=0)
    out[len(pieces) * RHS :] = to_int16(jnp.concatenate([rows, jnp.zeros_like(rows)], axis=1))


def decode(message, count):
    rows = message[count * RHS :].astype(jnp.int32).astype(F32)[:, :RHS]
    square = jnp.concatenate([rows, jnp.zeros((RHS - EXTRA, RHS), F32)], axis=0).T
    pieces = []
    for m in range(count):
        scale = size_of(square[:, m : m + 1]) * (1.0 / FULL)
        pieces.append(message[m * RHS : (m + 1) * RHS].astype(jnp.int32).astype(F32) * scale)
    return pieces


def two_rows(rows):
    return jnp.concatenate([rows[0], rows[1], jnp.zeros((6, RHS), F32)], axis=0)


def live_pair(live, leaf_a, leaf_b):
    return jnp.concatenate([live[pl.ds(leaf_a, 1), :], live[pl.ds(leaf_b, 1), :]], axis=1)


def first_message(data, extra, out):
    out[:RHS] = data[...].T.astype(BF16)
    out[RHS:] = extra[...]


M_ROW, M_HALO, M_OWNER, M_AT, M_ODD, M_COL = 16, 24, 26, 27, 28, 29


def slot_of(meta, column):
    apart = column ^ meta[M_AT]
    swapped = (apart % 4) * 4 + apart // 4
    return jnp.where(meta[M_ODD] == 1, swapped, apart)


def tile_at(tiles, s, k):
    return tiles[s % 4][BAND * (s // 4) + k]


def data_pieces(group, other):
    return [a[:RHS] for a in group] + [other[MSG * m : MSG * m + RHS] for m in range(4)]


def data_extras(group, other):
    return [a[RHS:] for a in group] + [other[MSG * m + RHS : MSG * (m + 1)] for m in range(4)]


def add_near_terms(meta, cols, pieces, tiles, near):
    near[...] = jnp.zeros_like(near)

    @pl.when(meta[M_OWNER] == 1)
    def _():
        for s in range(COLS):
            for k in range(BAND):
                slot = slot_of(meta, cols[s, k])
                near[slot] += nn(pieces[s], tile_at(tiles, s, k))


def far_pair(meta, live, left, right, pieces, slot):
    ja, jb = meta[slot], meta[slot + 1]
    coef_a, coef_b, right_a, right_b = [], [], [], []
    for s in range(COLS):
        base = meta[M_ROW + s] * ROWS
        pair = jnp.concatenate([left[base + ja], left[base + jb]], axis=0)
        coef = (nt(pieces[s], pair) * live_pair(live, base + ja, base + jb)).astype(BF16)
        coef_a.append(coef[:, :RANK])
        coef_b.append(coef[:, RANK:])
        right_a.append(right[base + ja])
        right_b.append(right[base + jb])
    part_a = nn(jnp.concatenate(coef_a, axis=1), jnp.concatenate(right_a, axis=0))
    part_b = nn(jnp.concatenate(coef_b, axis=1), jnp.concatenate(right_b, axis=0))
    return part_a, part_b


def far_group(meta, live, left, right, pieces, m2):
    first = far_pair(meta, live, left, right, pieces, 4 * m2)
    return first + far_pair(meta, live, left, right, pieces, 4 * m2 + 2)


def far_only_kernel(meta, live, left, right, a0, a1, a2, a3, b, far, cols):
    pieces = data_pieces((a0, a1, a2, a3), b)
    rows = [extra.astype(F32)[:1, :RHS] for extra in data_extras((a0, a1, a2, a3), b)]
    cols[...] = jnp.concatenate(rows, axis=0).astype(jnp.int32)
    for m2 in range(4):
        for m1, part in enumerate(far_group(meta, live, left, right, pieces, m2)):
            far[4 * m2 + m1] = part


def near_encode_kernel(meta, cols, far, a0, a1, a2, a3, b, t0, t1, t2, t3, g1, g3, g2, own_out, near):
    add_near_terms(meta, cols, data_pieces((a0, a1, a2, a3), b), (t0, t1, t2, t3), near)
    zero = jnp.zeros((1, RHS), F32)
    for m2, out in ((1, g1), (3, g3), (2, g2)):
        encode(out, [far[4 * m2 + m] + near[4 * m2 + m] for m in range(4)], [zero, zero])
    for m in range(4):
        own_out[m * RHS : (m + 1) * RHS] = far[m] + near[m]


def adjoint_first_kernel(
    meta, cols, reg, live, left, right, a0, a1, a2, a3, b, t0, t1, t2, t3, g1, g3, g2, near, sums_out, rims_out, first, last
):
    pieces = data_pieces((a0, a1, a2, a3), b)
    sums = [jnp.zeros((1, RHS), F32)] * 2
    for s, extra in enumerate(data_extras((a0, a1, a2, a3), b)):
        terms = extra.astype(F32)[:, :RHS]
        sums = [sums[0] + (terms[0:1] + terms[1:2] + terms[2:3]), sums[1] + (terms[3:4] + terms[4:5] + terms[5:6])]
        column = meta[M_ROW + s]
        first[pl.ds(column, 1), :] = terms[6:7]
        last[pl.ds(column, 1), :] = terms[7:8]
    at, column = meta[M_AT], meta[M_COL]
    cross = jnp.sum(last[0 : COLS - 1] * first[1:COLS], axis=0, keepdims=True)
    sums[1] += jnp.where(at == 0, -2.0 * reg[...] * cross, 0.0)
    before = last[pl.ds(jnp.maximum(column - 1, 0), 1), :]
    after = first[pl.ds(jnp.minimum(column + 1, COLS - 1), 1), :]
    rims_out[...] = two_rows(
        [
            jnp.where(column > 0, before, 0.0),
            jnp.where(column < COLS - 1, after, 0.0),
        ]
    )
    sums_out[...] = two_rows(sums)
    add_near_terms(meta, cols, pieces, (t0, t1, t2, t3), near)
    for m2, out in ((1, g1), (3, g3), (2, g2)):
        parts = far_group(meta, live, left, right, pieces, m2)
        encode(out, [part + near[4 * m2 + m] for m, part in enumerate(parts)], sums)


def adjoint_second_kernel(meta, live, left, right, a0, a1, a2, a3, b, near, own_out):
    pieces = data_pieces((a0, a1, a2, a3), b)
    for m, part in enumerate(far_group(meta, live, left, right, pieces, 0)):
        own_out[m * RHS : (m + 1) * RHS] = part + near[m]


def coefficient_pair(meta, live, right, held, s, slots):
    base_a, base_b = meta[M_ROW + s] * ROWS, meta[M_ROW + s + 1] * ROWS
    coef_a, coef_b = [], []
    for slot in slots:
        j = meta[slot]
        pair = jnp.concatenate([right[base_a + j], right[base_b + j]], axis=0)
        coef = (nt(held(slot), pair) * live_pair(live, base_a + j, base_b + j)).astype(BF16)
        coef_a.append(coef[:, :RANK])
        coef_b.append(coef[:, RANK:])
    return jnp.concatenate(coef_a, axis=1), jnp.concatenate(coef_b, axis=1)


def piece_of(arrays):
    def held(slot):
        return arrays[slot // 4][(slot % 4) * RHS : (slot % 4 + 1) * RHS]

    return held


def left_rows(meta, left, s, slots):
    base = meta[M_ROW + s] * ROWS
    return jnp.concatenate([left[base + meta[slot]] for slot in slots], axis=0)


def forward_near_kernel(meta, live, left, right, a, partial):
    for s in (4, 6, 0, 2):
        for at, coef in enumerate(coefficient_pair(meta, live, right, piece_of((a,)), s, range(4))):
            partial[s + at] = nn(coef, left_rows(meta, left, s + at, range(4)))


def forward_rows(meta, cols, live, left, right, partial, arrays, tiles, out, near, held, start):
    piece = piece_of(arrays)
    for slot in range(ROWS):
        held[slot] = piece(slot)
    for m in range(4):
        near[m] = partial[start + m]

    @pl.when(meta[M_OWNER] == 1)
    def _():
        for m in range(4):
            for k in range(BAND):
                slot = slot_of(meta, cols[start + m, k])
                near[m] += nt(held[slot], tile_at(tiles, start + m, k))

    for m in (0, 2):
        s = start + m
        for at, coef in enumerate(coefficient_pair(meta, live, right, piece, s, range(4, ROWS))):
            value = nn(coef, left_rows(meta, left, s + at, range(4, ROWS))) + near[m + at]
            out[(m + at) * RHS : (m + at + 1) * RHS] = value.astype(out.dtype)


def forward_first_kernel(
    meta, cols, live, left, right, partial, a, b1, b2, b3, t0, t1, t2, t3, out, held, near
):
    forward_rows(
        meta, cols, live, left, right, partial, (a, b1, b2, b3), (t0, t1, t2, t3), out, near, held, 4
    )


def forward_second_kernel(
    meta, cols, live, left, right, partial, a, b1, b2, b3, t0, t1, t2, t3, own, out, curved, edges, held, near
):
    forward_rows(
        meta, cols, live, left, right, partial, (a, b1, b2, b3), (t0, t1, t2, t3), out, near, held, 0
    )
    lane = lax.broadcasted_iota(jnp.int32, (RHS, LEAF), 1)
    for m in range(4):
        rows = slice(m * RHS, (m + 1) * RHS)
        vector, j = own[rows], meta[m]
        before = held[slot_of(meta, (j + ROWS - 1) % ROWS)][:, LEAF - RHS :].astype(F32)[:, RHS - 1 :]
        after = held[slot_of(meta, (j + 1) % ROWS)][:, :RHS].astype(F32)[:, :1]
        before = jnp.where(j == 0, 0.0, before)
        after = jnp.where(j == ROWS - 1, 0.0, after)
        below = jnp.where(lane == 0, before, pltpu.roll(vector, 1, 1))
        above = jnp.where(lane == LEAF - 1, after, pltpu.roll(vector, LEAF - 1, 1))
        curved[rows] = 2.0 * vector - below - above
    first = held[slot_of(meta, 0)][:, :RHS].astype(F32).T[:1]
    last = held[slot_of(meta, ROWS - 1)][:, LEAF - RHS :].astype(F32).T[RHS - 1 :]
    edges[...] = two_rows([first, last])


def without_rims(curved, before, after, j):
    lane = lax.broadcasted_iota(jnp.int32, (RHS, LEAF), 1)
    curved = curved - jnp.where((lane == 0) & (j == 0), before, 0.0)
    return curved - jnp.where((lane == LEAF - 1) & (j == ROWS - 1), after, 0.0)


def row_phase_kernel(own, sums_in, g1, g3, g2, own_out, sums_out, message):
    sums = [sums_in[0:1], sums_in[1:2]]
    totals = [own[m * RHS : (m + 1) * RHS] for m in range(4)]
    for g in (g1, g3, g2):
        sums = [x + y for x, y in zip(sums, decode_rows(g[4 * RHS :]))]
        totals = [x + y for x, y in zip(totals, decode(g, 4))]
    sums_out[...] = two_rows(sums)
    encode(message, totals, sums)
    for m in range(4):
        own_out[m * RHS : (m + 1) * RHS] = totals[m]


def group_totals(own, p1, p3, p2):
    totals = [own[m * RHS : (m + 1) * RHS] for m in range(4)]
    for k, p in ((1, p1), (3, p3), (2, p2)):
        got = decode(p, 4)
        totals = [total + got[k ^ m] for m, total in enumerate(totals)]
    return totals


def descent_kernel(own, p1, p3, p2, full, sent):
    for m, total in enumerate(group_totals(own, p1, p3, p2)):
        full[m * RHS : (m + 1) * RHS] = total
        sent[m * RHS : (m + 1) * RHS] = total.astype(BF16)


def descent2_kernel(meta, reg, first, curved, rims, own, sums_in, p1, p3, p2, full, sent, curved_out, sums_out):
    sums = [sums_in[0:1], sums_in[1:2]]
    for p in (p1, p3, p2):
        sums = [x + y for x, y in zip(sums, decode_rows(p[4 * RHS :]))]
    sums_out[...] = two_rows(sums)
    step, weight = as_column(sums[0] / sums[1]), as_column(reg[...])
    before, after = as_column(rims[0:1]), as_column(rims[1:2])
    for m, total in enumerate(group_totals(own, p1, p3, p2)):
        rows = slice(m * RHS, (m + 1) * RHS)
        whole = without_rims(curved[rows], before, after, meta[m])
        curved_out[rows] = whole
        vector = first[rows] - step * (total + weight * whole)
        full[rows] = vector
        sent[rows] = vector.astype(BF16)


def core_phase_kernel(own, other, own_out, p1, p3, p2):
    for m, out in ((1, p1), (3, p3), (2, p2), (0, own_out)):
        rows = slice(m * RHS, (m + 1) * RHS)
        out[...] = (own[rows] + other[rows].astype(F32)).astype(out.dtype)


def image_kernel(reg, vector, curved, edges, own, p1, p3, p2, full, message):
    total = own[...]
    for p in (p1, p3, p2):
        total += p[...].astype(F32)
    full[...] = total
    value = vector[:RHS]
    message[:RHS] = total.astype(BF16)
    gamma = row_sum(value * value)
    delta = row_sum(total * total) + reg[...] * row_sum(value * curved[:RHS])
    rows = jnp.concatenate(
        split3(gamma) + split3(delta) + [edges[0:2], jnp.zeros((EXTRA - 8, RHS), F32)], axis=0
    )
    message[RHS:] = jnp.concatenate([rows, jnp.zeros_like(rows)], axis=1).astype(BF16)


def image2_kernel(meta, reg, vector, curved, edges, curved_first, first, own, p1, p3, p2, full, sums):
    total = own[...]
    for p in (p1, p3, p2):
        total += p[...].astype(F32)
    full[...] = total
    value = vector[:RHS]
    weight = reg[...]
    sums[...] = jnp.zeros_like(sums)
    sums[0:1] = row_sum(value * value)
    sums[1:2] = row_sum(total * total) + weight * row_sum(value * curved[:RHS])
    sums[2:3] = row_sum(total * first[...]) + weight * row_sum(value * curved_first[:RHS])
    column = meta[M_COL]
    sums[pl.ds(8 + column, 1), :] = jnp.where(meta[M_AT] == 0, edges[0:1], 0.0)
    sums[pl.ds(16 + column, 1), :] = jnp.where(meta[M_AT] == 0, edges[1:2], 0.0)


def transposed_kernel(*refs):
    sources, near, outs, (held, sems) = refs[:4], refs[4:6], refs[6:12], refs[12:]
    copies = [
        pltpu.make_async_copy(source.at[pl.ds(0, RHS)], held.at[k], sems.at[k]) for k, source in enumerate(sources)
    ]
    for copy in copies:
        copy.start()
    for value, out in zip(near, outs[4:]):
        out[...] = value[...].T
    for k, copy in enumerate(copies):
        copy.wait()
        outs[k][...] = held[k].T


def final_kernel(meta, reg, sums1, gathered, s1, s2, d1, d2, y1, y2, data, solution_out, misfit_out, curved_out, held):
    total = gathered[:SUMS]
    for k in range(1, ROWS):
        total += gathered[k * SUMS : (k + 1) * SUMS]
    held[...] = total
    gamma, delta = sums1[0:1], sums1[1:2]
    first, last = held[8 : 8 + COLS], held[16 : 16 + COLS]
    cross = jnp.sum(last[: COLS - 1] * first[1:], axis=0, keepdims=True)
    fresh, delta_new, delta_mixed = held[0:1], held[1:2] - 2.0 * reg[...] * cross, held[2:3]
    at, column = meta[M_AT], meta[M_COL]
    before = held[pl.ds(16 + jnp.maximum(column - 1, 0), 1), :]
    after = held[pl.ds(8 + jnp.minimum(column + 1, COLS - 1), 1), :]
    row = lax.broadcasted_iota(jnp.int32, (LEAF, RHS), 0)
    curved = d2[...] - jnp.where((row == 0) & (at == 0) & (column > 0), before, 0.0)
    curved -= jnp.where((row == LEAF - 1) & (at == ROWS - 1) & (column < COLS - 1), after, 0.0)
    beta = fresh / gamma
    delta2 = delta_new + 2.0 * beta * delta_mixed + beta * beta * delta
    two = fresh / delta2
    one = gamma / delta + two * beta
    solution_out[...] = one * s1[...] + two * s2[...]
    curved_out[...] = one * d1[...] + two * curved
    misfit_out[...] = data[...] - (one * y1[...] + two * y2[...])


def grid_pairs(move):
    return [(r * COLS + c, to) for r in range(ROWS) for c in range(COLS) for to in [move(r, c)] if to is not None]


def send(value, move):
    return lax.ppermute(value, ("row", "col"), grid_pairs(move))


def near_move(m):
    return lambda r, c: (r ^ (m if c % 2 == 0 else 4 * m)) * COLS + c


def far_move(m):
    return lambda r, c: (r ^ (4 * m if c % 2 == 0 else m)) * COLS + c


def y_move(m):
    return lambda r, c: r * COLS + (c ^ (2 * m))


def core_move(r, c):
    return r * COLS + (c ^ 1)


def tile_core_move(r, c):
    return r * COLS + (c ^ 1) if c % 2 != (r // 2) % 2 else None


def tile_move(m):
    def move(r, c):
        owner = r // 2
        there = c % 2 == owner % 2 and (c // 2) ^ (owner // 2) == m
        return r * COLS + (c ^ (2 * m)) if there else None

    return move


def per_device(far_left, far_right, far_rank, near_tiles, near_cols, data, reg_weight):
    r = lax.axis_index("row")
    c = lax.axis_index("col")
    odd = c % 2
    leaves = far_rank.shape[-1]

    def at_slot(m2, m1):
        return jnp.where(odd == 0, r ^ m1 ^ (4 * m2), r ^ (4 * m1) ^ m2)

    def slot_at(column):
        apart = column ^ r
        return jnp.where(odd == 1, (apart % 4) * 4 + apart // 4, apart)

    meta = jnp.stack(
        [at_slot(s // 4, s % 4) for s in range(ROWS)]
        + [c ^ (2 * (s % 4)) ^ (s // 4) for s in range(COLS)]
        + [slot_at((r + ROWS - 1) % ROWS), slot_at((r + 1) % ROWS)]
        + [(c == r // 2).astype(jnp.int32), r, odd, c]
    ).astype(jnp.int32)
    reg = reg_weight.reshape(1, RHS)
    data = data.reshape(LEAF, RHS)

    cols_row = jnp.pad(near_cols.astype(BF16), ((0, EXTRA - 1), (0, LEAF - BAND)))
    message = call(first_message, shape((MSG, LEAF), BF16), data, cols_row)

    def gather_col_pieces(mine):
        got = {m: send(mine, y_move(m)) for m in ORDER}
        return [mine, got[1], got[2], got[3]]

    group = gather_col_pieces(message)
    tiles, _ = lax.optimization_barrier((near_tiles.reshape(BAND, LEAF, LEAF), message))
    tiles = jnp.concatenate([tiles, send(tiles, tile_core_move)], axis=0)
    tiles = [tiles] + [send(tiles, tile_move(m)) for m in (1, 2, 3)]
    left = far_left.reshape(leaves, RANK, LEAF)
    right = far_right.reshape(leaves, RANK, LEAF)
    live = (lax.broadcasted_iota(jnp.int32, (leaves, RANK), 1) < far_rank.reshape(leaves, 1)).astype(F32)
    other = send(jnp.concatenate(group, axis=0), core_move)

    def factors():
        return [live] + [pltpu.with_memory_space_constraint(x, pltpu.VMEM) for x in (left, right)]

    vec, sums_shape = shape((RHS, LEAF)), shape((8, RHS))
    sent_shape = shape((RHS, LEAF), BF16)
    group4, group4_sent = shape((4 * RHS, LEAF)), shape((4 * RHS, LEAF), BF16)
    big = shape((4 * RHS + EXTRA, LEAF), jnp.int16)
    near_shape = shape((ROWS, RHS, LEAF))
    near_scratch = pltpu.VMEM((ROWS, RHS, LEAF), F32)

    def specs(scalars, vectors):
        return [SMEM] * scalars + [VMEM] * vectors

    def sum_over_row(own, sums, parts):
        got = [send(g, far_move(m)) for m, g in zip(ORDER, parts)]
        own, sums, message = call(row_phase_kernel, (group4, sums_shape, big), own, sums, *got)
        return own, sums, [send(message, near_move(m)) for m in ORDER]

    def product(vector, sent):
        got = {m: send(sent, far_move(m)) for m in ORDER}
        pieces = [sent, got[1], got[2], got[3]]
        partial = call(
            forward_near_kernel, shape((COLS, RHS, LEAF)), meta, *factors(), sent, specs=specs(1, 4), flops=1 << 29
        )
        scratch = [pltpu.VMEM((ROWS, RHS, LEAF), BF16), pltpu.VMEM((4, RHS, LEAF), F32)]
        parts = call(
            forward_first_kernel, group4_sent, meta, cols, *factors(), partial, *pieces, *tiles,
            specs=specs(2, 12), scratch=scratch, flops=1 << 30,
        )
        other = send(parts, core_move)
        own, curved, edges = call(
            forward_second_kernel, (group4, group4, sums_shape), meta, cols, *factors(), partial, *pieces, *tiles, vector,
            specs=specs(2, 13), scratch=scratch, flops=1 << 30,
        )
        own, p1, p3, p2 = call(core_phase_kernel, (vec, sent_shape, sent_shape, sent_shape), own, other)
        return curved, edges, [own] + [send(p, y_move(m)) for m, p in zip(ORDER, (p1, p3, p2))]

    far, cols = call(
        far_only_kernel, (near_shape, shape((COLS, RHS), jnp.int32)), meta, *factors(), *group, other,
        specs=specs(1, 8), flops=1 << 32,
    )
    g1, g3, g2, own = call(
        near_encode_kernel, (big, big, big, group4), meta, cols, far, *group, other, *tiles,
        specs=specs(2, 10), scratch=[near_scratch], flops=1 << 29,
    )
    own, _, parts = sum_over_row(own, jnp.zeros((8, RHS), F32), (g1, g3, g2))
    s1, s1_sent = call(descent_kernel, (group4, group4_sent), own, *parts)
    d1, edges, parts = product(s1, s1_sent)
    y1, message = call(image_kernel, (vec, shape((MSG, LEAF), BF16)), reg, s1, d1, edges, *parts)

    group = gather_col_pieces(message)
    other = send(jnp.concatenate(group, axis=0), core_move)
    g1, g3, g2, near, sums, rims = call(
        adjoint_first_kernel, (big, big, big, near_shape, sums_shape, sums_shape),
        meta, cols, reg, *factors(), *group, other, *tiles,
        specs=specs(2, 13), scratch=[pltpu.VMEM((COLS, RHS), F32)] * 2, flops=1 << 30,
    )
    own = call(
        adjoint_second_kernel, group4, meta, *factors(), *group, other, near,
        specs=specs(1, 9), flops=1 << 30,
    )
    own, sums, parts = sum_over_row(own, sums, (g1, g3, g2))
    s2, s2_sent, d1, sums1 = call(
        descent2_kernel, (group4, group4_sent, group4, sums_shape), meta, reg, s1, d1, rims, own, sums, *parts,
        specs=specs(1, 9),
    )
    d2, edges, parts = product(s2, s2_sent)
    y2, sums2 = call(
        image2_kernel, (vec, shape((SUMS, RHS))), meta, reg, s2, d2, edges, d1, y1, *parts, specs=specs(1, 10)
    )
    sums2 = sums2 + send(sums2, core_move)
    got = {m: send(sums2, y_move(m)) for m in ORDER}
    sums2 = (sums2 + got[1]) + (got[2] + got[3])
    gathered = lax.all_to_all(jnp.tile(sums2, (ROWS, 1)), "row", 0, 0, tiled=True)
    piece = shape((LEAF, RHS))
    in_hbm = [pltpu.with_memory_space_constraint(x, pltpu.HBM) for x in (s1, s2, d1, d2)]
    ready = call(
        transposed_kernel, (piece,) * 6, *in_hbm, y1, y2, specs=[HBM] * 4 + [VMEM] * 2,
        scratch=[pltpu.VMEM((4, RHS, LEAF), F32), pltpu.SemaphoreType.DMA((4,))],
    )
    solution_out, misfit_out, curved_out = call(
        final_kernel, (piece, piece, piece), meta, reg, sums1, gathered, *ready, data,
        specs=specs(1, 10), scratch=[pltpu.VMEM((SUMS, RHS), F32)],
    )
    whole = (1, 1, LEAF, RHS)
    return solution_out.reshape(whole), misfit_out.reshape(whole), curved_out.reshape(whole)


def solution(mesh):
    in_specs = (
        P("row", "col", None, None, None),
        P("row", "col", None, None, None),
        P("row", "col", None),
        P(("row", "col"), None, None, None),
        P(("row", "col"), None),
        P("row", "col", None, None),
        P(),
    )
    out_specs = (
        P("col", "row", None, None),
        P("row", "col", None, None),
        P("col", "row", None, None),
    )
    return jax.shard_map(
        per_device, mesh=mesh, in_specs=in_specs, out_specs=out_specs, check_vma=False
    )
```

```python
import jax
import jax.numpy as jnp
from jax import lax
from jax.experimental import pallas as pl
from jax.experimental.pallas import tpu as pltpu
from jax.sharding import PartitionSpec as P

F32 = jnp.float32
BF16 = jnp.bfloat16
ROWS = 16
COLS = 8
RANK = 128
RHS = 128
LEAF = 256
BAND = 3
EXTRA = 16
MSG = RHS + EXTRA
ORDER = (1, 3, 2)
SUMS = 24
FULL = 32000.0
VMEM = pl.BlockSpec(memory_space=pltpu.VMEM)
SMEM = pl.BlockSpec(memory_space=pltpu.SMEM)
HBM = pl.BlockSpec(memory_space=pl.ANY)


def shape(dims, dtype=F32):
    return jax.ShapeDtypeStruct(dims, dtype)


def call(kernel, outs, *args, specs=None, scratch=(), limit=8, flops=0):
    return pl.pallas_call(
        kernel,
        out_shape=outs,
        in_specs=specs or [VMEM] * len(args),
        out_specs=jax.tree.map(lambda _: VMEM, outs),
        scratch_shapes=list(scratch),
        compiler_params=pltpu.CompilerParams(vmem_limit_bytes=limit << 20),
        cost_estimate=pl.CostEstimate(flops=flops, bytes_accessed=1 << 16, transcendentals=0),
    )(*args)


def nt(left, right):
    return lax.dot_general(left, right, (((1,), (1,)), ((), ())), preferred_element_type=F32)


def nn(left, right):
    return jnp.dot(left, right, preferred_element_type=F32)


def row_sum(values):
    folded = values[:, :RHS] + values[:, RHS:]
    return jnp.sum(folded.T, axis=0, keepdims=True)


def as_column(row):
    square = jnp.broadcast_to(row, (RHS, RHS)).T
    return jnp.concatenate([square, square], axis=1)


def split3(row):
    high = row.astype(BF16).astype(F32)
    middle = (row - high).astype(BF16).astype(F32)
    return [high, middle, row - high - middle]


def code_of(largest):
    return jnp.ceil(jnp.log2(jnp.maximum(largest, 1e-30)) * 128.0)


def size_of(code):
    return jnp.exp2(code * (1.0 / 128.0))


def to_int16(values):
    return jnp.round(values).astype(jnp.int32).astype(jnp.int16)


def encode_rows(sums):
    rows = []
    for value in sums:
        code = code_of(jnp.abs(value))
        scaled = value / size_of(code) * FULL
        whole = jnp.round(scaled)
        rows += [code, whole, jnp.round((scaled - whole) * 65000.0)]
    return rows


def decode_rows(extra):
    rows = extra[...].astype(jnp.int32).astype(F32)[:, :RHS]
    sums = []
    for at in (4, 7):
        whole = rows[at + 1 : at + 2] + rows[at + 2 : at + 3] * (1.0 / 65000.0)
        sums.append(size_of(rows[at : at + 1]) * whole * (1.0 / FULL))
    return sums


def encode(out, pieces, sums):
    lane = lax.broadcasted_iota(jnp.int32, (RHS, RHS), 1)
    codes = jnp.zeros((RHS, RHS), F32)
    for m, piece in enumerate(pieces):
        code = code_of(jnp.max(jnp.abs(piece), axis=1, keepdims=True))
        out[m * RHS : (m + 1) * RHS] = to_int16(piece * (FULL / size_of(code)))
        codes = jnp.where(lane == m, code, codes)
    rows = jnp.concatenate([codes.T[:4]] + encode_rows(sums) + [jnp.zeros((EXTRA - 10, RHS), F32)], axis=0)
    out[len(pieces) * RHS :] = to_int16(jnp.concatenate([rows, jnp.zeros_like(rows)], axis=1))


def decode(message, count):
    rows = message[count * RHS :].astype(jnp.int32).astype(F32)[:, :RHS]
    square = jnp.concatenate([rows, jnp.zeros((RHS - EXTRA, RHS), F32)], axis=0).T
    pieces = []
    for m in range(count):
        scale = size_of(square[:, m : m + 1]) * (1.0 / FULL)
        pieces.append(message[m * RHS : (m + 1) * RHS].astype(jnp.int32).astype(F32) * scale)
    return pieces


def two_rows(rows):
    return jnp.concatenate([rows[0], rows[1], jnp.zeros((6, RHS), F32)], axis=0)


def live_pair(live, leaf_a, leaf_b):
    return jnp.concatenate([live[pl.ds(leaf_a, 1), :], live[pl.ds(leaf_b, 1), :]], axis=1)


def first_message(data, extra, out):
    out[:RHS] = data[...].T.astype(BF16)
    out[RHS:] = extra[...]


M_ROW, M_HALO, M_OWNER, M_AT, M_ODD, M_COL = 16, 24, 26, 27, 28, 29


def slot_of(meta, column):
    apart = column ^ meta[M_AT]
    swapped = (apart % 4) * 4 + apart // 4
    return jnp.where(meta[M_ODD] == 1, swapped, apart)


def tile_at(tiles, s, k):
    return tiles[s % 4][BAND * (s // 4) + k]


def data_pieces(group, other):
    return [a[:RHS] for a in group] + [other[MSG * m : MSG * m + RHS] for m in range(4)]


def data_extras(group, other):
    return [a[RHS:] for a in group] + [other[MSG * m + RHS : MSG * (m + 1)] for m in range(4)]


def add_near_terms(meta, cols, pieces, tiles, near):
    near[...] = jnp.zeros_like(near)

    @pl.when(meta[M_OWNER] == 1)
    def _():
        for s in range(COLS):
            for k in range(BAND):
                slot = slot_of(meta, cols[s, k])
                near[slot] += nn(pieces[s], tile_at(tiles, s, k))


def far_pair(meta, live, left, right, pieces, slot):
    ja, jb = meta[slot], meta[slot + 1]
    coef_a, coef_b, right_a, right_b = [], [], [], []
    for s in range(COLS):
        base = meta[M_ROW + s] * ROWS
        pair = jnp.concatenate([left[base + ja], left[base + jb]], axis=0)
        coef = (nt(pieces[s], pair) * live_pair(live, base + ja, base + jb)).astype(BF16)
        coef_a.append(coef[:, :RANK])
        coef_b.append(coef[:, RANK:])
        right_a.append(right[base + ja])
        right_b.append(right[base + jb])
    part_a = nn(jnp.concatenate(coef_a, axis=1), jnp.concatenate(right_a, axis=0))
    part_b = nn(jnp.concatenate(coef_b, axis=1), jnp.concatenate(right_b, axis=0))
    return part_a, part_b


def far_group(meta, live, left, right, pieces, m2):
    first = far_pair(meta, live, left, right, pieces, 4 * m2)
    return first + far_pair(meta, live, left, right, pieces, 4 * m2 + 2)


def far_only_kernel(meta, live, left, right, a0, a1, a2, a3, b, far, cols):
    pieces = data_pieces((a0, a1, a2, a3), b)
    rows = [extra.astype(F32)[:1, :RHS] for extra in data_extras((a0, a1, a2, a3), b)]
    cols[...] = jnp.concatenate(rows, axis=0).astype(jnp.int32)
    for m2 in range(4):
        for m1, part in enumerate(far_group(meta, live, left, right, pieces, m2)):
            far[4 * m2 + m1] = part


def near_encode_kernel(meta, cols, far, a0, a1, a2, a3, b, t0, t1, t2, t3, g1, g3, g2, own_out, near):
    add_near_terms(meta, cols, data_pieces((a0, a1, a2, a3), b), (t0, t1, t2, t3), near)
    zero = jnp.zeros((1, RHS), F32)
    for m2, out in ((1, g1), (3, g3), (2, g2)):
        encode(out, [far[4 * m2 + m] + near[4 * m2 + m] for m in range(4)], [zero, zero])
    for m in range(4):
        own_out[m * RHS : (m + 1) * RHS] = far[m] + near[m]


def adjoint_first_kernel(
    meta, cols, reg, live, left, right, a0, a1, a2, a3, b, t0, t1, t2, t3, g1, g3, g2, near, sums_out, rims_out, first, last
):
    pieces = data_pieces((a0, a1, a2, a3), b)
    sums = [jnp.zeros((1, RHS), F32)] * 2
    for s, extra in enumerate(data_extras((a0, a1, a2, a3), b)):
        terms = extra.astype(F32)[:, :RHS]
        sums = [sums[0] + (terms[0:1] + terms[1:2] + terms[2:3]), sums[1] + (terms[3:4] + terms[4:5] + terms[5:6])]
        column = meta[M_ROW + s]
        first[pl.ds(column, 1), :] = terms[6:7]
        last[pl.ds(column, 1), :] = terms[7:8]
    at, column = meta[M_AT], meta[M_COL]
    cross = jnp.sum(last[0 : COLS - 1] * first[1:COLS], axis=0, keepdims=True)
    sums[1] += jnp.where(at == 0, -2.0 * reg[...] * cross, 0.0)
    before = last[pl.ds(jnp.maximum(column - 1, 0), 1), :]
    after = first[pl.ds(jnp.minimum(column + 1, COLS - 1), 1), :]
    rims_out[...] = two_rows(
        [
            jnp.where(column > 0, before, 0.0),
            jnp.where(column < COLS - 1, after, 0.0),
        ]
    )
    sums_out[...] = two_rows(sums)
    add_near_terms(meta, cols, pieces, (t0, t1, t2, t3), near)
    for m2, out in ((1, g1), (3, g3), (2, g2)):
        parts = far_group(meta, live, left, right, pieces, m2)
        encode(out, [part + near[4 * m2 + m] for m, part in enumerate(parts)], sums)


def adjoint_second_kernel(meta, live, left, right, a0, a1, a2, a3, b, near, own_out):
    pieces = data_pieces((a0, a1, a2, a3), b)
    for m, part in enumerate(far_group(meta, live, left, right, pieces, 0)):
        own_out[m * RHS : (m + 1) * RHS] = part + near[m]


def coefficient_pair(meta, live, right, held, s, slots):
    base_a, base_b = meta[M_ROW + s] * ROWS, meta[M_ROW + s + 1] * ROWS
    coef_a, coef_b = [], []
    for slot in slots:
        j = meta[slot]
        pair = jnp.concatenate([right[base_a + j], right[base_b + j]], axis=0)
        coef = (nt(held(slot), pair) * live_pair(live, base_a + j, base_b + j)).astype(BF16)
        coef_a.append(coef[:, :RANK])
        coef_b.append(coef[:, RANK:])
    return jnp.concatenate(coef_a, axis=1), jnp.concatenate(coef_b, axis=1)


def piece_of(arrays):
    def held(slot):
        return arrays[slot // 4][(slot % 4) * RHS : (slot % 4 + 1) * RHS]

    return held


def left_rows(meta, left, s, slots):
    base = meta[M_ROW + s] * ROWS
    return jnp.concatenate([left[base + meta[slot]] for slot in slots], axis=0)


def forward_near_kernel(meta, live, left, right, a, partial):
    for s in (4, 6, 0, 2):
        for at, coef in enumerate(coefficient_pair(meta, live, right, piece_of((a,)), s, range(4))):
            partial[s + at] = nn(coef, left_rows(meta, left, s + at, range(4)))


def forward_rows(meta, cols, live, left, right, partial, arrays, tiles, out, near, held, start):
    piece = piece_of(arrays)
    for slot in range(ROWS):
        held[slot] = piece(slot)
    for m in range(4):
        near[m] = partial[start + m]

    @pl.when(meta[M_OWNER] == 1)
    def _():
        for m in range(4):
            for k in range(BAND):
                slot = slot_of(meta, cols[start + m, k])
                near[m] += nt(held[slot], tile_at(tiles, start + m, k))

    for m in (0, 2):
        s = start + m
        for at, coef in enumerate(coefficient_pair(meta, live, right, piece, s, range(4, ROWS))):
            value = nn(coef, left_rows(meta, left, s + at, range(4, ROWS))) + near[m + at]
            out[(m + at) * RHS : (m + at + 1) * RHS] = value.astype(out.dtype)


def forward_first_kernel(
    meta, cols, live, left, right, partial, a, b1, b2, b3, t0, t1, t2, t3, out, held, near
):
    forward_rows(
        meta, cols, live, left, right, partial, (a, b1, b2, b3), (t0, t1, t2, t3), out, near, held, 4
    )


def forward_second_kernel(
    meta, cols, live, left, right, partial, a, b1, b2, b3, t0, t1, t2, t3, own, out, curved, edges, held, near
):
    forward_rows(
        meta, cols, live, left, right, partial, (a, b1, b2, b3), (t0, t1, t2, t3), out, near, held, 0
    )
    lane = lax.broadcasted_iota(jnp.int32, (RHS, LEAF), 1)
    for m in range(4):
        rows = slice(m * RHS, (m + 1) * RHS)
        vector, j = own[rows], meta[m]
        before = held[slot_of(meta, (j + ROWS - 1) % ROWS)][:, LEAF - RHS :].astype(F32)[:, RHS - 1 :]
        after = held[slot_of(meta, (j + 1) % ROWS)][:, :RHS].astype(F32)[:, :1]
        before = jnp.where(j == 0, 0.0, before)
        after = jnp.where(j == ROWS - 1, 0.0, after)
        below = jnp.where(lane == 0, before, pltpu.roll(vector, 1, 1))
        above = jnp.where(lane == LEAF - 1, after, pltpu.roll(vector, LEAF - 1, 1))
        curved[rows] = 2.0 * vector - below - above
    first = held[slot_of(meta, 0)][:, :RHS].astype(F32).T[:1]
    last = held[slot_of(meta, ROWS - 1)][:, LEAF - RHS :].astype(F32).T[RHS - 1 :]
    edges[...] = two_rows([first, last])


def without_rims(curved, before, after, j):
    lane = lax.broadcasted_iota(jnp.int32, (RHS, LEAF), 1)
    curved = curved - jnp.where((lane == 0) & (j == 0), before, 0.0)
    return curved - jnp.where((lane == LEAF - 1) & (j == ROWS - 1), after, 0.0)


def row_phase_first_kernel(own, g1, g3, g2, own_out, message):
    totals = [own[m * RHS : (m + 1) * RHS] for m in range(4)]
    for g in (g1, g3, g2):
        totals = [x + y for x, y in zip(totals, decode(g, 4))]
    zero = jnp.zeros((1, RHS), F32)
    encode(message, totals, [zero, zero])
    for m in range(4):
        own_out[m * RHS : (m + 1) * RHS] = totals[m]


def row_phase_kernel(own, sums_in, g1, g3, g2, own_out, sums_out, message):
    sums = [sums_in[0:1], sums_in[1:2]]
    totals = [own[m * RHS : (m + 1) * RHS] for m in range(4)]
    for g in (g1, g3, g2):
        sums = [x + y for x, y in zip(sums, decode_rows(g[4 * RHS :]))]
        totals = [x + y for x, y in zip(totals, decode(g, 4))]
    sums_out[...] = two_rows(sums)
    encode(message, totals, sums)
    for m in range(4):
        own_out[m * RHS : (m + 1) * RHS] = totals[m]


def group_totals(own, p1, p3, p2):
    totals = [own[m * RHS : (m + 1) * RHS] for m in range(4)]
    for k, p in ((1, p1), (3, p3), (2, p2)):
        got = decode(p, 4)
        totals = [total + got[k ^ m] for m, total in enumerate(totals)]
    return totals


def descent_kernel(own, p1, p3, p2, full, sent):
    for m, total in enumerate(group_totals(own, p1, p3, p2)):
        full[m * RHS : (m + 1) * RHS] = total
        sent[m * RHS : (m + 1) * RHS] = total.astype(BF16)


def descent2_kernel(meta, reg, first, curved, rims, own, sums_in, p1, p3, p2, full, sent, curved_out, sums_out):
    sums = [sums_in[0:1], sums_in[1:2]]
    for p in (p1, p3, p2):
        sums = [x + y for x, y in zip(sums, decode_rows(p[4 * RHS :]))]
    sums_out[...] = two_rows(sums)
    step, weight = as_column(sums[0] / sums[1]), as_column(reg[...])
    before, after = as_column(rims[0:1]), as_column(rims[1:2])
    for m, total in enumerate(group_totals(own, p1, p3, p2)):
        rows = slice(m * RHS, (m + 1) * RHS)
        whole = without_rims(curved[rows], before, after, meta[m])
        curved_out[rows] = whole
        vector = first[rows] - step * (total + weight * whole)
        full[rows] = vector
        sent[rows] = vector.astype(BF16)


def core_phase_kernel(own, other, own_out, p1, p3, p2):
    for m, out in ((1, p1), (3, p3), (2, p2), (0, own_out)):
        rows = slice(m * RHS, (m + 1) * RHS)
        out[...] = (own[rows] + other[rows].astype(F32)).astype(out.dtype)


def image_kernel(reg, vector, curved, edges, own, p1, p3, p2, full, message):
    total = own[...]
    for p in (p1, p3, p2):
        total += p[...].astype(F32)
    full[...] = total
    value = vector[:RHS]
    message[:RHS] = total.astype(BF16)
    gamma = row_sum(value * value)
    delta = row_sum(total * total) + reg[...] * row_sum(value * curved[:RHS])
    rows = jnp.concatenate(
        split3(gamma) + split3(delta) + [edges[0:2], jnp.zeros((EXTRA - 8, RHS), F32)], axis=0
    )
    message[RHS:] = jnp.concatenate([rows, jnp.zeros_like(rows)], axis=1).astype(BF16)


def image2_kernel(meta, reg, vector, curved, edges, curved_first, first, own, p1, p3, p2, full, sums):
    total = own[...]
    for p in (p1, p3, p2):
        total += p[...].astype(F32)
    full[...] = total
    value = vector[:RHS]
    weight = reg[...]
    sums[...] = jnp.zeros_like(sums)
    sums[0:1] = row_sum(value * value)
    sums[1:2] = row_sum(total * total) + weight * row_sum(value * curved[:RHS])
    sums[2:3] = row_sum(total * first[...]) + weight * row_sum(value * curved_first[:RHS])
    column = meta[M_COL]
    sums[pl.ds(8 + column, 1), :] = jnp.where(meta[M_AT] == 0, edges[0:1], 0.0)
    sums[pl.ds(16 + column, 1), :] = jnp.where(meta[M_AT] == 0, edges[1:2], 0.0)


def repeat_kernel(own, p1, p3, p2, out):
    total = own[...] + p1[...] + (p3[...] + p2[...])
    for k in range(ROWS):
        out[k * SUMS : (k + 1) * SUMS] = total


def transposed_kernel(*refs):
    sources, near, outs, (held, sems) = refs[:4], refs[4:6], refs[6:12], refs[12:]
    copies = [
        pltpu.make_async_copy(source.at[pl.ds(0, RHS)], held.at[k], sems.at[k]) for k, source in enumerate(sources)
    ]
    for copy in copies:
        copy.start()
    for value, out in zip(near, outs[4:]):
        out[...] = value[...].T
    for k, copy in enumerate(copies):
        copy.wait()
        outs[k][...] = held[k].T


def final_kernel(meta, reg, sums1, gathered, s1, s2, d1, d2, y1, y2, data, solution_out, misfit_out, curved_out, held):
    total = gathered[:SUMS]
    for k in range(1, ROWS):
        total += gathered[k * SUMS : (k + 1) * SUMS]
    held[...] = total
    gamma, delta = sums1[0:1], sums1[1:2]
    first, last = held[8 : 8 + COLS], held[16 : 16 + COLS]
    cross = jnp.sum(last[: COLS - 1] * first[1:], axis=0, keepdims=True)
    fresh, delta_new, delta_mixed = held[0:1], held[1:2] - 2.0 * reg[...] * cross, held[2:3]
    at, column = meta[M_AT], meta[M_COL]
    before = held[pl.ds(16 + jnp.maximum(column - 1, 0), 1), :]
    after = held[pl.ds(8 + jnp.minimum(column + 1, COLS - 1), 1), :]
    row = lax.broadcasted_iota(jnp.int32, (LEAF, RHS), 0)
    curved = d2[...] - jnp.where((row == 0) & (at == 0) & (column > 0), before, 0.0)
    curved -= jnp.where((row == LEAF - 1) & (at == ROWS - 1) & (column < COLS - 1), after, 0.0)
    beta = fresh / gamma
    delta2 = delta_new + 2.0 * beta * delta_mixed + beta * beta * delta
    two = fresh / delta2
    one = gamma / delta + two * beta
    solution_out[...] = one * s1[...] + two * s2[...]
    curved_out[...] = one * d1[...] + two * curved
    misfit_out[...] = data[...] - (one * y1[...] + two * y2[...])


def grid_pairs(move):
    return [(r * COLS + c, to) for r in range(ROWS) for c in range(COLS) for to in [move(r, c)] if to is not None]


def send(value, move):
    return lax.ppermute(value, ("row", "col"), grid_pairs(move))


def near_move(m):
    return lambda r, c: (r ^ (m if c % 2 == 0 else 4 * m)) * COLS + c


def far_move(m):
    return lambda r, c: (r ^ (4 * m if c % 2 == 0 else m)) * COLS + c


def y_move(m):
    return lambda r, c: r * COLS + (c ^ (2 * m))


def core_move(r, c):
    return r * COLS + (c ^ 1)


def tile_core_move(r, c):
    return r * COLS + (c ^ 1) if c % 2 != (r // 2) % 2 else None


def tile_move(m):
    def move(r, c):
        owner = r // 2
        there = c % 2 == owner % 2 and (c // 2) ^ (owner // 2) == m
        return r * COLS + (c ^ (2 * m)) if there else None

    return move


def per_device(far_left, far_right, far_rank, near_tiles, near_cols, data, reg_weight):
    r = lax.axis_index("row")
    c = lax.axis_index("col")
    odd = c % 2
    leaves = far_rank.shape[-1]

    def at_slot(m2, m1):
        return jnp.where(odd == 0, r ^ m1 ^ (4 * m2), r ^ (4 * m1) ^ m2)

    def slot_at(column):
        apart = column ^ r
        return jnp.where(odd == 1, (apart % 4) * 4 + apart // 4, apart)

    meta = jnp.stack(
        [at_slot(s // 4, s % 4) for s in range(ROWS)]
        + [c ^ (2 * (s % 4)) ^ (s // 4) for s in range(COLS)]
        + [slot_at((r + ROWS - 1) % ROWS), slot_at((r + 1) % ROWS)]
        + [(c == r // 2).astype(jnp.int32), r, odd, c]
    ).astype(jnp.int32)
    reg = reg_weight.reshape(1, RHS)
    data = data.reshape(LEAF, RHS)

    cols_row = jnp.pad(near_cols.astype(BF16), ((0, EXTRA - 1), (0, LEAF - BAND)))
    message = call(first_message, shape((MSG, LEAF), BF16), data, cols_row)

    def gather_col_pieces(mine):
        got = {m: send(mine, y_move(m)) for m in ORDER}
        return [mine, got[1], got[2], got[3]]

    group = gather_col_pieces(message)
    tiles = near_tiles.reshape(BAND, LEAF, LEAF)
    tiles = jnp.concatenate([tiles, send(tiles, tile_core_move)], axis=0)
    tiles = [tiles] + [send(tiles, tile_move(m)) for m in (1, 2, 3)]
    left = far_left.reshape(leaves, RANK, LEAF)
    right = far_right.reshape(leaves, RANK, LEAF)
    live = (lax.broadcasted_iota(jnp.int32, (leaves, RANK), 1) < far_rank.reshape(leaves, 1)).astype(F32)
    other = send(jnp.concatenate(group, axis=0), core_move)

    def factors():
        return [live] + [pltpu.with_memory_space_constraint(x, pltpu.VMEM) for x in (left, right)]

    vec, sums_shape = shape((RHS, LEAF)), shape((8, RHS))
    sent_shape = shape((RHS, LEAF), BF16)
    group4, group4_sent = shape((4 * RHS, LEAF)), shape((4 * RHS, LEAF), BF16)
    big = shape((4 * RHS + EXTRA, LEAF), jnp.int16)
    near_shape = shape((ROWS, RHS, LEAF))
    near_scratch = pltpu.VMEM((ROWS, RHS, LEAF), F32)

    def specs(scalars, vectors):
        return [SMEM] * scalars + [VMEM] * vectors

    def sum_over_row(own, sums, parts):
        got = [send(g, far_move(m)) for m, g in zip(ORDER, parts)]
        if sums is None:
            own, message = call(row_phase_first_kernel, (group4, big), own, *got)
        else:
            own, sums, message = call(row_phase_kernel, (group4, sums_shape, big), own, sums, *got)
        return own, sums, [send(message, near_move(m)) for m in ORDER]

    def product(vector, sent):
        got = {m: send(sent, far_move(m)) for m in ORDER}
        pieces = [sent, got[1], got[2], got[3]]
        partial = call(
            forward_near_kernel, shape((COLS, RHS, LEAF)), meta, *factors(), sent, specs=specs(1, 4), flops=1 << 29
        )
        scratch = [pltpu.VMEM((ROWS, RHS, LEAF), BF16), pltpu.VMEM((4, RHS, LEAF), F32)]
        parts = call(
            forward_first_kernel, group4_sent, meta, cols, *factors(), partial, *pieces, *tiles,
            specs=specs(2, 12), scratch=scratch, flops=1 << 30,
        )
        other = send(parts, core_move)
        own, curved, edges = call(
            forward_second_kernel, (group4, group4, sums_shape), meta, cols, *factors(), partial, *pieces, *tiles, vector,
            specs=specs(2, 13), scratch=scratch, flops=1 << 30,
        )
        own, p1, p3, p2 = call(core_phase_kernel, (vec, sent_shape, sent_shape, sent_shape), own, other)
        return curved, edges, [own] + [send(p, y_move(m)) for m, p in zip(ORDER, (p1, p3, p2))]

    far, cols = call(
        far_only_kernel, (near_shape, shape((COLS, RHS), jnp.int32)), meta, *factors(), *group, other,
        specs=specs(1, 8), flops=1 << 32,
    )
    g1, g3, g2, own = call(
        near_encode_kernel, (big, big, big, group4), meta, cols, far, *group, other, *tiles,
        specs=specs(2, 10), scratch=[near_scratch], flops=1 << 29,
    )
    own, _, parts = sum_over_row(own, None, (g1, g3, g2))
    s1, s1_sent = call(descent_kernel, (group4, group4_sent), own, *parts)
    d1, edges, parts = product(s1, s1_sent)
    y1, message = call(image_kernel, (vec, shape((MSG, LEAF), BF16)), reg, s1, d1, edges, *parts)

    group = gather_col_pieces(message)
    other = send(jnp.concatenate(group, axis=0), core_move)
    g1, g3, g2, near, sums, rims = call(
        adjoint_first_kernel, (big, big, big, near_shape, sums_shape, sums_shape),
        meta, cols, reg, *factors(), *group, other, *tiles,
        specs=specs(2, 13), scratch=[pltpu.VMEM((COLS, RHS), F32)] * 2, flops=1 << 30,
    )
    own = call(
        adjoint_second_kernel, group4, meta, *factors(), *group, other, near,
        specs=specs(1, 9), flops=1 << 30,
    )
    own, sums, parts = sum_over_row(own, sums, (g1, g3, g2))
    s2, s2_sent, d1, sums1 = call(
        descent2_kernel, (group4, group4_sent, group4, sums_shape), meta, reg, s1, d1, rims, own, sums, *parts,
        specs=specs(1, 9),
    )
    d2, edges, parts = product(s2, s2_sent)
    y2, sums2 = call(
        image2_kernel, (vec, shape((SUMS, RHS))), meta, reg, s2, d2, edges, d1, y1, *parts, specs=specs(1, 10)
    )
    sums2 = sums2 + send(sums2, core_move)
    got = [send(sums2, y_move(m)) for m in ORDER]
    repeated = call(repeat_kernel, shape((ROWS * SUMS, RHS)), sums2, *got)
    gathered = lax.all_to_all(repeated, "row", 0, 0, tiled=True)
    piece = shape((LEAF, RHS))
    in_hbm = [pltpu.with_memory_space_constraint(x, pltpu.HBM) for x in (s1, s2, d1, d2)]
    ready = call(
        transposed_kernel, (piece,) * 6, *in_hbm, y1, y2, specs=[HBM] * 4 + [VMEM] * 2,
        scratch=[pltpu.VMEM((4, RHS, LEAF), F32), pltpu.SemaphoreType.DMA((4,))],
    )
    solution_out, misfit_out, curved_out = call(
        final_kernel, (piece, piece, piece), meta, reg, sums1, gathered, *ready, data,
        specs=specs(1, 10), scratch=[pltpu.VMEM((SUMS, RHS), F32)],
    )
    whole = (1, 1, LEAF, RHS)
    return solution_out.reshape(whole), misfit_out.reshape(whole), curved_out.reshape(whole)


def solution(mesh):
    in_specs = (
        P("row", "col", None, None, None),
        P("row", "col", None, None, None),
        P("row", "col", None),
        P(("row", "col"), None, None, None),
        P(("row", "col"), None),
        P("row", "col", None, None),
        P(),
    )
    out_specs = (
        P("col", "row", None, None),
        P("row", "col", None, None),
        P("col", "row", None, None),
    )
    return jax.shard_map(
        per_device, mesh=mesh, in_specs=in_specs, out_specs=out_specs, check_vma=False
    )
```

```python
import jax
import jax.numpy as jnp
from jax import lax
from jax.experimental import pallas as pl
from jax.experimental.pallas import tpu as pltpu
from jax.sharding import PartitionSpec as P

F32 = jnp.float32
BF16 = jnp.bfloat16
ROWS = 16
COLS = 8
RANK = 128
RHS = 128
LEAF = 256
BAND = 3
EXTRA = 16
MSG = RHS + EXTRA
ORDER = (1, 3, 2)
SUMS = 24
FULL = 32000.0
VMEM = pl.BlockSpec(memory_space=pltpu.VMEM)
SMEM = pl.BlockSpec(memory_space=pltpu.SMEM)
HBM = pl.BlockSpec(memory_space=pl.ANY)


def shape(dims, dtype=F32):
    return jax.ShapeDtypeStruct(dims, dtype)


def call(kernel, outs, *args, specs=None, scratch=(), limit=8, flops=0):
    return pl.pallas_call(
        kernel,
        out_shape=outs,
        in_specs=specs or [VMEM] * len(args),
        out_specs=jax.tree.map(lambda _: VMEM, outs),
        scratch_shapes=list(scratch),
        compiler_params=pltpu.CompilerParams(vmem_limit_bytes=limit << 20),
        cost_estimate=pl.CostEstimate(flops=flops, bytes_accessed=1 << 16, transcendentals=0),
    )(*args)


def nt(left, right):
    return lax.dot_general(left, right, (((1,), (1,)), ((), ())), preferred_element_type=F32)


def nn(left, right):
    return jnp.dot(left, right, preferred_element_type=F32)


def row_sum(values):
    folded = values[:, :RHS] + values[:, RHS:]
    return jnp.sum(folded.T, axis=0, keepdims=True)


def as_column(row):
    square = jnp.broadcast_to(row, (RHS, RHS)).T
    return jnp.concatenate([square, square], axis=1)


def split3(row):
    high = row.astype(BF16).astype(F32)
    middle = (row - high).astype(BF16).astype(F32)
    return [high, middle, row - high - middle]


def code_of(largest):
    return jnp.ceil(jnp.log2(jnp.maximum(largest, 1e-30)) * 128.0)


def size_of(code):
    return jnp.exp2(code * (1.0 / 128.0))


def to_int16(values):
    return jnp.round(values).astype(jnp.int32).astype(jnp.int16)


def encode_rows(sums):
    rows = []
    for value in sums:
        code = code_of(jnp.abs(value))
        scaled = value / size_of(code) * FULL
        whole = jnp.round(scaled)
        rows += [code, whole, jnp.round((scaled - whole) * 65000.0)]
    return rows


def decode_rows(extra):
    rows = extra[...].astype(jnp.int32).astype(F32)[:, :RHS]
    sums = []
    for at in (4, 7):
        whole = rows[at + 1 : at + 2] + rows[at + 2 : at + 3] * (1.0 / 65000.0)
        sums.append(size_of(rows[at : at + 1]) * whole * (1.0 / FULL))
    return sums


def encode(out, pieces, sums):
    lane = lax.broadcasted_iota(jnp.int32, (RHS, RHS), 1)
    codes = jnp.zeros((RHS, RHS), F32)
    for m, piece in enumerate(pieces):
        code = code_of(jnp.max(jnp.abs(piece), axis=1, keepdims=True))
        out[m * RHS : (m + 1) * RHS] = to_int16(piece * (FULL / size_of(code)))
        codes = jnp.where(lane == m, code, codes)
    rows = jnp.concatenate([codes.T[:4]] + encode_rows(sums) + [jnp.zeros((EXTRA - 10, RHS), F32)], axis=0)
    out[len(pieces) * RHS :] = to_int16(jnp.concatenate([rows, jnp.zeros_like(rows)], axis=1))


def decode(message, count):
    rows = message[count * RHS :].astype(jnp.int32).astype(F32)[:, :RHS]
    square = jnp.concatenate([rows, jnp.zeros((RHS - EXTRA, RHS), F32)], axis=0).T
    pieces = []
    for m in range(count):
        scale = size_of(square[:, m : m + 1]) * (1.0 / FULL)
        pieces.append(message[m * RHS : (m + 1) * RHS].astype(jnp.int32).astype(F32) * scale)
    return pieces


def two_rows(rows):
    return jnp.concatenate([rows[0], rows[1], jnp.zeros((6, RHS), F32)], axis=0)


def live_pair(live, leaf_a, leaf_b):
    return jnp.concatenate([live[pl.ds(leaf_a, 1), :], live[pl.ds(leaf_b, 1), :]], axis=1)


def first_message(data, extra, out):
    out[:RHS] = data[...].T.astype(BF16)
    out[RHS:] = extra[...]


M_ROW, M_HALO, M_OWNER, M_AT, M_ODD, M_COL = 16, 24, 26, 27, 28, 29


def slot_of(meta, column):
    apart = column ^ meta[M_AT]
    swapped = (apart % 4) * 4 + apart // 4
    return jnp.where(meta[M_ODD] == 1, swapped, apart)


def tile_at(tiles, s, k):
    return tiles[s % 4][BAND * (s // 4) + k]


def data_pieces(group, other):
    return [a[:RHS] for a in group] + [other[MSG * m : MSG * m + RHS] for m in range(4)]


def data_extras(group, other):
    return [a[RHS:] for a in group] + [other[MSG * m + RHS : MSG * (m + 1)] for m in range(4)]


def add_near_terms(meta, cols, pieces, tiles, near):
    near[...] = jnp.zeros_like(near)

    @pl.when(meta[M_OWNER] == 1)
    def _():
        for s in range(COLS):
            for k in range(BAND):
                slot = slot_of(meta, cols[s, k])
                near[slot] += nn(pieces[s], tile_at(tiles, s, k))


def far_pair(meta, live, left, right, pieces, slot):
    ja, jb = meta[slot], meta[slot + 1]
    coef_a, coef_b, right_a, right_b = [], [], [], []
    for s in range(COLS):
        base = meta[M_ROW + s] * ROWS
        pair = jnp.concatenate([left[base + ja], left[base + jb]], axis=0)
        coef = (nt(pieces[s], pair) * live_pair(live, base + ja, base + jb)).astype(BF16)
        coef_a.append(coef[:, :RANK])
        coef_b.append(coef[:, RANK:])
        right_a.append(right[base + ja])
        right_b.append(right[base + jb])
    part_a = nn(jnp.concatenate(coef_a, axis=1), jnp.concatenate(right_a, axis=0))
    part_b = nn(jnp.concatenate(coef_b, axis=1), jnp.concatenate(right_b, axis=0))
    return part_a, part_b


def far_group(meta, live, left, right, pieces, m2):
    first = far_pair(meta, live, left, right, pieces, 4 * m2)
    return first + far_pair(meta, live, left, right, pieces, 4 * m2 + 2)


def far_only_kernel(meta, live, left, right, a0, a1, a2, a3, b, far, cols):
    pieces = data_pieces((a0, a1, a2, a3), b)
    rows = [extra.astype(F32)[:1, :RHS] for extra in data_extras((a0, a1, a2, a3), b)]
    cols[...] = jnp.concatenate(rows, axis=0).astype(jnp.int32)
    for m2 in range(4):
        for m1, part in enumerate(far_group(meta, live, left, right, pieces, m2)):
            far[4 * m2 + m1] = part


def near_encode_kernel(meta, cols, far, a0, a1, a2, a3, b, t0, t1, t2, t3, g1, g3, g2, own_out, near):
    add_near_terms(meta, cols, data_pieces((a0, a1, a2, a3), b), (t0, t1, t2, t3), near)
    zero = jnp.zeros((1, RHS), F32)
    for m2, out in ((1, g1), (3, g3), (2, g2)):
        encode(out, [far[4 * m2 + m] + near[4 * m2 + m] for m in range(4)], [zero, zero])
    for m in range(4):
        own_out[m * RHS : (m + 1) * RHS] = far[m] + near[m]


def adjoint_first_kernel(
    meta, cols, reg, live, left, right, a0, a1, a2, a3, b, t0, t1, t2, t3, g1, g3, g2, near, sums_out, rims_out, first, last
):
    pieces = data_pieces((a0, a1, a2, a3), b)
    sums = [jnp.zeros((1, RHS), F32)] * 2
    for s, extra in enumerate(data_extras((a0, a1, a2, a3), b)):
        terms = extra.astype(F32)[:, :RHS]
        sums = [sums[0] + (terms[0:1] + terms[1:2] + terms[2:3]), sums[1] + (terms[3:4] + terms[4:5] + terms[5:6])]
        column = meta[M_ROW + s]
        first[pl.ds(column, 1), :] = terms[6:7]
        last[pl.ds(column, 1), :] = terms[7:8]
    at, column = meta[M_AT], meta[M_COL]
    cross = jnp.sum(last[0 : COLS - 1] * first[1:COLS], axis=0, keepdims=True)
    sums[1] += jnp.where(at == 0, -2.0 * reg[...] * cross, 0.0)
    before = last[pl.ds(jnp.maximum(column - 1, 0), 1), :]
    after = first[pl.ds(jnp.minimum(column + 1, COLS - 1), 1), :]
    rims_out[...] = two_rows(
        [
            jnp.where(column > 0, before, 0.0),
            jnp.where(column < COLS - 1, after, 0.0),
        ]
    )
    sums_out[...] = two_rows(sums)
    add_near_terms(meta, cols, pieces, (t0, t1, t2, t3), near)
    for m2, out in ((1, g1), (3, g3), (2, g2)):
        parts = far_group(meta, live, left, right, pieces, m2)
        encode(out, [part + near[4 * m2 + m] for m, part in enumerate(parts)], sums)


def adjoint_second_kernel(meta, live, left, right, a0, a1, a2, a3, b, near, own_out):
    pieces = data_pieces((a0, a1, a2, a3), b)
    for m, part in enumerate(far_group(meta, live, left, right, pieces, 0)):
        own_out[m * RHS : (m + 1) * RHS] = part + near[m]


def coefficient_pair(meta, live, right, held, s, slots):
    base_a, base_b = meta[M_ROW + s] * ROWS, meta[M_ROW + s + 1] * ROWS
    coef_a, coef_b = [], []
    for slot in slots:
        j = meta[slot]
        pair = jnp.concatenate([right[base_a + j], right[base_b + j]], axis=0)
        coef = (nt(held(slot), pair) * live_pair(live, base_a + j, base_b + j)).astype(BF16)
        coef_a.append(coef[:, :RANK])
        coef_b.append(coef[:, RANK:])
    return jnp.concatenate(coef_a, axis=1), jnp.concatenate(coef_b, axis=1)


def piece_of(arrays):
    def held(slot):
        return arrays[slot // 4][(slot % 4) * RHS : (slot % 4 + 1) * RHS]

    return held


def left_rows(meta, left, s, slots):
    base = meta[M_ROW + s] * ROWS
    return jnp.concatenate([left[base + meta[slot]] for slot in slots], axis=0)


def forward_near_kernel(meta, live, left, right, a, partial):
    for s in (4, 6, 0, 2):
        for at, coef in enumerate(coefficient_pair(meta, live, right, piece_of((a,)), s, range(4))):
            partial[s + at] = nn(coef, left_rows(meta, left, s + at, range(4)))


def forward_rows(meta, cols, live, left, right, partial, arrays, tiles, out, near, held, start):
    piece = piece_of(arrays)
    for slot in range(ROWS):
        held[slot] = piece(slot)
    for m in range(4):
        near[m] = partial[start + m]

    @pl.when(meta[M_OWNER] == 1)
    def _():
        for m in range(4):
            chosen = [held[slot_of(meta, cols[start + m, k])] for k in range(BAND)]
            band = [tile_at(tiles, start + m, k) for k in range(BAND)]
            near[m] += nt(jnp.concatenate(chosen, axis=1), jnp.concatenate(band, axis=1))

    for m in (0, 2):
        s = start + m
        for at, coef in enumerate(coefficient_pair(meta, live, right, piece, s, range(4, ROWS))):
            value = nn(coef, left_rows(meta, left, s + at, range(4, ROWS))) + near[m + at]
            out[(m + at) * RHS : (m + at + 1) * RHS] = value.astype(out.dtype)


def forward_first_kernel(
    meta, cols, live, left, right, partial, a, b1, b2, b3, t0, t1, t2, t3, out, held, near
):
    forward_rows(
        meta, cols, live, left, right, partial, (a, b1, b2, b3), (t0, t1, t2, t3), out, near, held, 4
    )


def forward_second_kernel(
    meta, cols, live, left, right, partial, a, b1, b2, b3, t0, t1, t2, t3, own, out, curved, edges, held, near
):
    forward_rows(
        meta, cols, live, left, right, partial, (a, b1, b2, b3), (t0, t1, t2, t3), out, near, held, 0
    )
    lane = lax.broadcasted_iota(jnp.int32, (RHS, LEAF), 1)
    for m in range(4):
        rows = slice(m * RHS, (m + 1) * RHS)
        vector, j = own[rows], meta[m]
        before = held[slot_of(meta, (j + ROWS - 1) % ROWS)][:, LEAF - RHS :].astype(F32)[:, RHS - 1 :]
        after = held[slot_of(meta, (j + 1) % ROWS)][:, :RHS].astype(F32)[:, :1]
        before = jnp.where(j == 0, 0.0, before)
        after = jnp.where(j == ROWS - 1, 0.0, after)
        below = jnp.where(lane == 0, before, pltpu.roll(vector, 1, 1))
        above = jnp.where(lane == LEAF - 1, after, pltpu.roll(vector, LEAF - 1, 1))
        curved[rows] = 2.0 * vector - below - above
    first = held[slot_of(meta, 0)][:, :RHS].astype(F32).T[:1]
    last = held[slot_of(meta, ROWS - 1)][:, LEAF - RHS :].astype(F32).T[RHS - 1 :]
    edges[...] = two_rows([first, last])


def without_rims(curved, before, after, j):
    lane = lax.broadcasted_iota(jnp.int32, (RHS, LEAF), 1)
    curved = curved - jnp.where((lane == 0) & (j == 0), before, 0.0)
    return curved - jnp.where((lane == LEAF - 1) & (j == ROWS - 1), after, 0.0)


def row_phase_first_kernel(own, g1, g3, g2, own_out, message):
    totals = [own[m * RHS : (m + 1) * RHS] for m in range(4)]
    for g in (g1, g3, g2):
        totals = [x + y for x, y in zip(totals, decode(g, 4))]
    zero = jnp.zeros((1, RHS), F32)
    encode(message, totals, [zero, zero])
    for m in range(4):
        own_out[m * RHS : (m + 1) * RHS] = totals[m]


def row_phase_kernel(own, sums_in, g1, g3, g2, own_out, sums_out, message):
    sums = [sums_in[0:1], sums_in[1:2]]
    totals = [own[m * RHS : (m + 1) * RHS] for m in range(4)]
    for g in (g1, g3, g2):
        sums = [x + y for x, y in zip(sums, decode_rows(g[4 * RHS :]))]
        totals = [x + y for x, y in zip(totals, decode(g, 4))]
    sums_out[...] = two_rows(sums)
    encode(message, totals, sums)
    for m in range(4):
        own_out[m * RHS : (m + 1) * RHS] = totals[m]


def group_totals(own, p1, p3, p2):
    totals = [own[m * RHS : (m + 1) * RHS] for m in range(4)]
    for k, p in ((1, p1), (3, p3), (2, p2)):
        got = decode(p, 4)
        totals = [total + got[k ^ m] for m, total in enumerate(totals)]
    return totals


def descent_kernel(own, p1, p3, p2, full, sent):
    for m, total in enumerate(group_totals(own, p1, p3, p2)):
        full[m * RHS : (m + 1) * RHS] = total
        sent[m * RHS : (m + 1) * RHS] = total.astype(BF16)


def descent2_kernel(meta, reg, first, curved, rims, own, sums_in, p1, p3, p2, full, sent, curved_out, sums_out):
    sums = [sums_in[0:1], sums_in[1:2]]
    for p in (p1, p3, p2):
        sums = [x + y for x, y in zip(sums, decode_rows(p[4 * RHS :]))]
    sums_out[...] = two_rows(sums)
    step, weight = as_column(sums[0] / sums[1]), as_column(reg[...])
    before, after = as_column(rims[0:1]), as_column(rims[1:2])
    for m, total in enumerate(group_totals(own, p1, p3, p2)):
        rows = slice(m * RHS, (m + 1) * RHS)
        whole = without_rims(curved[rows], before, after, meta[m])
        curved_out[rows] = whole
        vector = first[rows] - step * (total + weight * whole)
        full[rows] = vector
        sent[rows] = vector.astype(BF16)


def core_phase_kernel(own, other, own_out, p1, p3, p2):
    for m, out in ((1, p1), (3, p3), (2, p2), (0, own_out)):
        rows = slice(m * RHS, (m + 1) * RHS)
        out[...] = (own[rows] + other[rows].astype(F32)).astype(out.dtype)


def image_kernel(reg, vector, curved, edges, own, p1, p3, p2, full, message):
    total = own[...]
    for p in (p1, p3, p2):
        total += p[...].astype(F32)
    full[...] = total
    value = vector[:RHS]
    message[:RHS] = total.astype(BF16)
    gamma = row_sum(value * value)
    delta = row_sum(total * total) + reg[...] * row_sum(value * curved[:RHS])
    rows = jnp.concatenate(
        split3(gamma) + split3(delta) + [edges[0:2], jnp.zeros((EXTRA - 8, RHS), F32)], axis=0
    )
    message[RHS:] = jnp.concatenate([rows, jnp.zeros_like(rows)], axis=1).astype(BF16)


def image2_kernel(meta, reg, vector, curved, edges, curved_first, first, own, p1, p3, p2, full, sums):
    total = own[...]
    for p in (p1, p3, p2):
        total += p[...].astype(F32)
    full[...] = total
    value = vector[:RHS]
    weight = reg[...]
    sums[...] = jnp.zeros_like(sums)
    sums[0:1] = row_sum(value * value)
    sums[1:2] = row_sum(total * total) + weight * row_sum(value * curved[:RHS])
    sums[2:3] = row_sum(total * first[...]) + weight * row_sum(value * curved_first[:RHS])
    column = meta[M_COL]
    sums[pl.ds(8 + column, 1), :] = jnp.where(meta[M_AT] == 0, edges[0:1], 0.0)
    sums[pl.ds(16 + column, 1), :] = jnp.where(meta[M_AT] == 0, edges[1:2], 0.0)


def repeat_kernel(own, p1, p3, p2, out):
    total = own[...] + p1[...] + (p3[...] + p2[...])
    for k in range(ROWS):
        out[k * SUMS : (k + 1) * SUMS] = total


def transposed_kernel(*refs):
    sources, near, outs, (held, sems) = refs[:4], refs[4:6], refs[6:12], refs[12:]
    copies = [
        pltpu.make_async_copy(source.at[pl.ds(0, RHS)], held.at[k], sems.at[k]) for k, source in enumerate(sources)
    ]
    for copy in copies:
        copy.start()
    for value, out in zip(near, outs[4:]):
        out[...] = value[...].T
    for k, copy in enumerate(copies):
        copy.wait()
        outs[k][...] = held[k].T


def final_kernel(meta, reg, sums1, gathered, s1, s2, d1, d2, y1, y2, data, solution_out, misfit_out, curved_out, held):
    total = gathered[:SUMS]
    for k in range(1, ROWS):
        total += gathered[k * SUMS : (k + 1) * SUMS]
    held[...] = total
    gamma, delta = sums1[0:1], sums1[1:2]
    first, last = held[8 : 8 + COLS], held[16 : 16 + COLS]
    cross = jnp.sum(last[: COLS - 1] * first[1:], axis=0, keepdims=True)
    fresh, delta_new, delta_mixed = held[0:1], held[1:2] - 2.0 * reg[...] * cross, held[2:3]
    at, column = meta[M_AT], meta[M_COL]
    before = held[pl.ds(16 + jnp.maximum(column - 1, 0), 1), :]
    after = held[pl.ds(8 + jnp.minimum(column + 1, COLS - 1), 1), :]
    row = lax.broadcasted_iota(jnp.int32, (LEAF, RHS), 0)
    curved = d2[...] - jnp.where((row == 0) & (at == 0) & (column > 0), before, 0.0)
    curved -= jnp.where((row == LEAF - 1) & (at == ROWS - 1) & (column < COLS - 1), after, 0.0)
    beta = fresh / gamma
    delta2 = delta_new + 2.0 * beta * delta_mixed + beta * beta * delta
    two = fresh / delta2
    one = gamma / delta + two * beta
    solution_out[...] = one * s1[...] + two * s2[...]
    curved_out[...] = one * d1[...] + two * curved
    misfit_out[...] = data[...] - (one * y1[...] + two * y2[...])


def grid_pairs(move):
    return [(r * COLS + c, to) for r in range(ROWS) for c in range(COLS) for to in [move(r, c)] if to is not None]


def send(value, move):
    return lax.ppermute(value, ("row", "col"), grid_pairs(move))


def near_move(m):
    return lambda r, c: (r ^ (m if c % 2 == 0 else 4 * m)) * COLS + c


def far_move(m):
    return lambda r, c: (r ^ (4 * m if c % 2 == 0 else m)) * COLS + c


def y_move(m):
    return lambda r, c: r * COLS + (c ^ (2 * m))


def core_move(r, c):
    return r * COLS + (c ^ 1)


def tile_core_move(r, c):
    return r * COLS + (c ^ 1) if c % 2 != (r // 2) % 2 else None


def tile_move(m):
    def move(r, c):
        owner = r // 2
        there = c % 2 == owner % 2 and (c // 2) ^ (owner // 2) == m
        return r * COLS + (c ^ (2 * m)) if there else None

    return move


def per_device(far_left, far_right, far_rank, near_tiles, near_cols, data, reg_weight):
    r = lax.axis_index("row")
    c = lax.axis_index("col")
    odd = c % 2
    leaves = far_rank.shape[-1]

    def at_slot(m2, m1):
        return jnp.where(odd == 0, r ^ m1 ^ (4 * m2), r ^ (4 * m1) ^ m2)

    def slot_at(column):
        apart = column ^ r
        return jnp.where(odd == 1, (apart % 4) * 4 + apart // 4, apart)

    meta = jnp.stack(
        [at_slot(s // 4, s % 4) for s in range(ROWS)]
        + [c ^ (2 * (s % 4)) ^ (s // 4) for s in range(COLS)]
        + [slot_at((r + ROWS - 1) % ROWS), slot_at((r + 1) % ROWS)]
        + [(c == r // 2).astype(jnp.int32), r, odd, c]
    ).astype(jnp.int32)
    reg = reg_weight.reshape(1, RHS)
    data = data.reshape(LEAF, RHS)

    cols_row = jnp.pad(near_cols.astype(BF16), ((0, EXTRA - 1), (0, LEAF - BAND)))
    message = call(first_message, shape((MSG, LEAF), BF16), data, cols_row)

    def gather_col_pieces(mine):
        got = {m: send(mine, y_move(m)) for m in ORDER}
        return [mine, got[1], got[2], got[3]]

    group = gather_col_pieces(message)
    tiles = near_tiles.reshape(BAND, LEAF, LEAF)
    tiles = jnp.concatenate([tiles, send(tiles, tile_core_move)], axis=0)
    tiles = [tiles] + [send(tiles, tile_move(m)) for m in (1, 2, 3)]
    left = far_left.reshape(leaves, RANK, LEAF)
    right = far_right.reshape(leaves, RANK, LEAF)
    live = (lax.broadcasted_iota(jnp.int32, (leaves, RANK), 1) < far_rank.reshape(leaves, 1)).astype(F32)
    other = send(jnp.concatenate(group, axis=0), core_move)

    def factors():
        return [live] + [pltpu.with_memory_space_constraint(x, pltpu.VMEM) for x in (left, right)]

    vec, sums_shape = shape((RHS, LEAF)), shape((8, RHS))
    sent_shape = shape((RHS, LEAF), BF16)
    group4, group4_sent = shape((4 * RHS, LEAF)), shape((4 * RHS, LEAF), BF16)
    big = shape((4 * RHS + EXTRA, LEAF), jnp.int16)
    near_shape = shape((ROWS, RHS, LEAF))
    near_scratch = pltpu.VMEM((ROWS, RHS, LEAF), F32)

    def specs(scalars, vectors):
        return [SMEM] * scalars + [VMEM] * vectors

    def sum_over_row(own, sums, parts):
        got = [send(g, far_move(m)) for m, g in zip(ORDER, parts)]
        if sums is None:
            own, message = call(row_phase_first_kernel, (group4, big), own, *got)
        else:
            own, sums, message = call(row_phase_kernel, (group4, sums_shape, big), own, sums, *got)
        return own, sums, [send(message, near_move(m)) for m in ORDER]

    def product(vector, sent):
        got = {m: send(sent, far_move(m)) for m in ORDER}
        pieces = [sent, got[1], got[2], got[3]]
        partial = call(
            forward_near_kernel, shape((COLS, RHS, LEAF)), meta, *factors(), sent, specs=specs(1, 4), flops=1 << 29
        )
        scratch = [pltpu.VMEM((ROWS, RHS, LEAF), BF16), pltpu.VMEM((4, RHS, LEAF), F32)]
        parts = call(
            forward_first_kernel, group4_sent, meta, cols, *factors(), partial, *pieces, *tiles,
            specs=specs(2, 12), scratch=scratch, flops=1 << 30,
        )
        other = send(parts, core_move)
        own, curved, edges = call(
            forward_second_kernel, (group4, group4, sums_shape), meta, cols, *factors(), partial, *pieces, *tiles, vector,
            specs=specs(2, 13), scratch=scratch, flops=1 << 30,
        )
        own, p1, p3, p2 = call(core_phase_kernel, (vec, sent_shape, sent_shape, sent_shape), own, other)
        return curved, edges, [own] + [send(p, y_move(m)) for m, p in zip(ORDER, (p1, p3, p2))]

    far, cols = call(
        far_only_kernel, (near_shape, shape((COLS, RHS), jnp.int32)), meta, *factors(), *group, other,
        specs=specs(1, 8), flops=1 << 32,
    )
    g1, g3, g2, own = call(
        near_encode_kernel, (big, big, big, group4), meta, cols, far, *group, other, *tiles,
        specs=specs(2, 10), scratch=[near_scratch], flops=1 << 29,
    )
    own, _, parts = sum_over_row(own, None, (g1, g3, g2))
    s1, s1_sent = call(descent_kernel, (group4, group4_sent), own, *parts)
    d1, edges, parts = product(s1, s1_sent)
    y1, message = call(image_kernel, (vec, shape((MSG, LEAF), BF16)), reg, s1, d1, edges, *parts)

    group = gather_col_pieces(message)
    other = send(jnp.concatenate(group, axis=0), core_move)
    g1, g3, g2, near, sums, rims = call(
        adjoint_first_kernel, (big, big, big, near_shape, sums_shape, sums_shape),
        meta, cols, reg, *factors(), *group, other, *tiles,
        specs=specs(2, 13), scratch=[pltpu.VMEM((COLS, RHS), F32)] * 2, flops=1 << 30,
    )
    own = call(
        adjoint_second_kernel, group4, meta, *factors(), *group, other, near,
        specs=specs(1, 9), flops=1 << 30,
    )
    own, sums, parts = sum_over_row(own, sums, (g1, g3, g2))
    s2, s2_sent, d1, sums1 = call(
        descent2_kernel, (group4, group4_sent, group4, sums_shape), meta, reg, s1, d1, rims, own, sums, *parts,
        specs=specs(1, 9),
    )
    d2, edges, parts = product(s2, s2_sent)
    y2, sums2 = call(
        image2_kernel, (vec, shape((SUMS, RHS))), meta, reg, s2, d2, edges, d1, y1, *parts, specs=specs(1, 10)
    )
    sums2 = sums2 + send(sums2, core_move)
    got = [send(sums2, y_move(m)) for m in ORDER]
    repeated = call(repeat_kernel, shape((ROWS * SUMS, RHS)), sums2, *got)
    gathered = lax.all_to_all(repeated, "row", 0, 0, tiled=True)
    piece = shape((LEAF, RHS))
    in_hbm = [pltpu.with_memory_space_constraint(x, pltpu.HBM) for x in (s1, s2, d1, d2)]
    ready = call(
        transposed_kernel, (piece,) * 6, *in_hbm, y1, y2, specs=[HBM] * 4 + [VMEM] * 2,
        scratch=[pltpu.VMEM((4, RHS, LEAF), F32), pltpu.SemaphoreType.DMA((4,))],
    )
    solution_out, misfit_out, curved_out = call(
        final_kernel, (piece, piece, piece), meta, reg, sums1, gathered, *ready, data,
        specs=specs(1, 10), scratch=[pltpu.VMEM((SUMS, RHS), F32)],
    )
    whole = (1, 1, LEAF, RHS)
    return solution_out.reshape(whole), misfit_out.reshape(whole), curved_out.reshape(whole)


def solution(mesh):
    in_specs = (
        P("row", "col", None, None, None),
        P("row", "col", None, None, None),
        P("row", "col", None),
        P(("row", "col"), None, None, None),
        P(("row", "col"), None),
        P("row", "col", None, None),
        P(),
    )
    out_specs = (
        P("col", "row", None, None),
        P("row", "col", None, None),
        P("col", "row", None, None),
    )
    return jax.shard_map(
        per_device, mesh=mesh, in_specs=in_specs, out_specs=out_specs, check_vma=False
    )
```

```python
import jax
import jax.numpy as jnp
from jax import lax
from jax.experimental import pallas as pl
from jax.experimental.pallas import tpu as pltpu
from jax.sharding import PartitionSpec as P

F32 = jnp.float32
BF16 = jnp.bfloat16
ROWS = 16
COLS = 8
RANK = 128
RHS = 128
LEAF = 256
BAND = 3
EXTRA = 16
MSG = RHS + EXTRA
ORDER = (1, 3, 2)
SUMS = 24
FULL = 32000.0
VMEM = pl.BlockSpec(memory_space=pltpu.VMEM)
SMEM = pl.BlockSpec(memory_space=pltpu.SMEM)
HBM = pl.BlockSpec(memory_space=pl.ANY)


def shape(dims, dtype=F32):
    return jax.ShapeDtypeStruct(dims, dtype)


def call(kernel, outs, *args, specs=None, scratch=(), limit=8, flops=0):
    return pl.pallas_call(
        kernel,
        out_shape=outs,
        in_specs=specs or [VMEM] * len(args),
        out_specs=jax.tree.map(lambda _: VMEM, outs),
        scratch_shapes=list(scratch),
        compiler_params=pltpu.CompilerParams(vmem_limit_bytes=limit << 20),
        cost_estimate=pl.CostEstimate(flops=flops, bytes_accessed=1 << 16, transcendentals=0),
    )(*args)


def nt(left, right):
    return lax.dot_general(left, right, (((1,), (1,)), ((), ())), preferred_element_type=F32)


def nn(left, right):
    return jnp.dot(left, right, preferred_element_type=F32)


def row_sum(values):
    folded = values[:, :RHS] + values[:, RHS:]
    return jnp.sum(folded.T, axis=0, keepdims=True)


def as_column(row):
    square = jnp.broadcast_to(row, (RHS, RHS)).T
    return jnp.concatenate([square, square], axis=1)


def split3(row):
    high = row.astype(BF16).astype(F32)
    middle = (row - high).astype(BF16).astype(F32)
    return [high, middle, row - high - middle]


def code_of(largest):
    return jnp.ceil(jnp.log2(jnp.maximum(largest, 1e-30)) * 128.0)


def size_of(code):
    return jnp.exp2(code * (1.0 / 128.0))


def to_int16(values):
    return jnp.round(values).astype(jnp.int32).astype(jnp.int16)


def encode_rows(sums):
    rows = []
    for value in sums:
        code = code_of(jnp.abs(value))
        scaled = value / size_of(code) * FULL
        whole = jnp.round(scaled)
        rows += [code, whole, jnp.round((scaled - whole) * 65000.0)]
    return rows


def decode_rows(extra):
    rows = extra[...].astype(jnp.int32).astype(F32)[:, :RHS]
    sums = []
    for at in (4, 7):
        whole = rows[at + 1 : at + 2] + rows[at + 2 : at + 3] * (1.0 / 65000.0)
        sums.append(size_of(rows[at : at + 1]) * whole * (1.0 / FULL))
    return sums


def encode(out, pieces, sums):
    lane = lax.broadcasted_iota(jnp.int32, (RHS, RHS), 1)
    codes = jnp.zeros((RHS, RHS), F32)
    for m, piece in enumerate(pieces):
        code = code_of(jnp.max(jnp.abs(piece), axis=1, keepdims=True))
        out[m * RHS : (m + 1) * RHS] = to_int16(piece * (FULL / size_of(code)))
        codes = jnp.where(lane == m, code, codes)
    rows = jnp.concatenate([codes.T[:4]] + encode_rows(sums) + [jnp.zeros((EXTRA - 10, RHS), F32)], axis=0)
    out[len(pieces) * RHS :] = to_int16(jnp.concatenate([rows, jnp.zeros_like(rows)], axis=1))


def decode(message, count):
    rows = message[count * RHS :].astype(jnp.int32).astype(F32)[:, :RHS]
    square = jnp.concatenate([rows, jnp.zeros((RHS - EXTRA, RHS), F32)], axis=0).T
    pieces = []
    for m in range(count):
        scale = size_of(square[:, m : m + 1]) * (1.0 / FULL)
        pieces.append(message[m * RHS : (m + 1) * RHS].astype(jnp.int32).astype(F32) * scale)
    return pieces


def two_rows(rows):
    return jnp.concatenate([rows[0], rows[1], jnp.zeros((6, RHS), F32)], axis=0)


def live_pair(live, leaf_a, leaf_b):
    return jnp.concatenate([live[pl.ds(leaf_a, 1), :], live[pl.ds(leaf_b, 1), :]], axis=1)


def first_message(data, extra, out):
    out[:RHS] = data[...].T.astype(BF16)
    out[RHS:] = extra[...]


M_ROW, M_HALO, M_OWNER, M_AT, M_ODD, M_COL = 16, 24, 26, 27, 28, 29


def slot_of(meta, column):
    apart = column ^ meta[M_AT]
    swapped = (apart % 4) * 4 + apart // 4
    return jnp.where(meta[M_ODD] == 1, swapped, apart)


def tile_at(tiles, s, k):
    return tiles[s % 4][BAND * (s // 4) + k]


def data_pieces(group, other):
    return [a[:RHS] for a in group] + [other[MSG * m : MSG * m + RHS] for m in range(4)]


def data_extras(group, other):
    return [a[RHS:] for a in group] + [other[MSG * m + RHS : MSG * (m + 1)] for m in range(4)]


def add_near_terms(meta, cols, pieces, tiles, near):
    near[...] = jnp.zeros_like(near)

    @pl.when(meta[M_OWNER] == 1)
    def _():
        for s in range(COLS):
            for k in range(BAND):
                slot = slot_of(meta, cols[s, k])
                near[slot] += nn(pieces[s], tile_at(tiles, s, k))


def far_pair(meta, live, left, right, pieces, slot):
    ja, jb = meta[slot], meta[slot + 1]
    coef_a, coef_b, right_a, right_b = [], [], [], []
    for s in range(COLS):
        base = meta[M_ROW + s] * ROWS
        pair = jnp.concatenate([left[base + ja], left[base + jb]], axis=0)
        coef = (nt(pieces[s], pair) * live_pair(live, base + ja, base + jb)).astype(BF16)
        coef_a.append(coef[:, :RANK])
        coef_b.append(coef[:, RANK:])
        right_a.append(right[base + ja])
        right_b.append(right[base + jb])
    part_a = nn(jnp.concatenate(coef_a, axis=1), jnp.concatenate(right_a, axis=0))
    part_b = nn(jnp.concatenate(coef_b, axis=1), jnp.concatenate(right_b, axis=0))
    return part_a, part_b


def far_group(meta, live, left, right, pieces, m2):
    first = far_pair(meta, live, left, right, pieces, 4 * m2)
    return first + far_pair(meta, live, left, right, pieces, 4 * m2 + 2)


def far_only_kernel(meta, live, left, right, a0, a1, a2, a3, b, far, cols):
    pieces = data_pieces((a0, a1, a2, a3), b)
    rows = [extra.astype(F32)[:1, :RHS] for extra in data_extras((a0, a1, a2, a3), b)]
    cols[...] = jnp.concatenate(rows, axis=0).astype(jnp.int32)
    for m2 in range(4):
        for m1, part in enumerate(far_group(meta, live, left, right, pieces, m2)):
            far[4 * m2 + m1] = part


def near_encode_kernel(meta, cols, far, a0, a1, a2, a3, b, t0, t1, t2, t3, g1, g3, g2, own_out, near):
    add_near_terms(meta, cols, data_pieces((a0, a1, a2, a3), b), (t0, t1, t2, t3), near)
    zero = jnp.zeros((1, RHS), F32)
    for m2, out in ((1, g1), (3, g3), (2, g2)):
        encode(out, [far[4 * m2 + m] + near[4 * m2 + m] for m in range(4)], [zero, zero])
    for m in range(4):
        own_out[m * RHS : (m + 1) * RHS] = far[m] + near[m]


def adjoint_first_kernel(
    meta, cols, reg, live, left, right, a0, a1, a2, a3, b, t0, t1, t2, t3, g1, g3, g2, near, sums_out, rims_out, first, last
):
    pieces = data_pieces((a0, a1, a2, a3), b)
    sums = [jnp.zeros((1, RHS), F32)] * 2
    for s, extra in enumerate(data_extras((a0, a1, a2, a3), b)):
        terms = extra.astype(F32)[:, :RHS]
        sums = [sums[0] + (terms[0:1] + terms[1:2] + terms[2:3]), sums[1] + (terms[3:4] + terms[4:5] + terms[5:6])]
        column = meta[M_ROW + s]
        first[pl.ds(column, 1), :] = terms[6:7]
        last[pl.ds(column, 1), :] = terms[7:8]
    at, column = meta[M_AT], meta[M_COL]
    cross = jnp.sum(last[0 : COLS - 1] * first[1:COLS], axis=0, keepdims=True)
    sums[1] += jnp.where(at == 0, -2.0 * reg[...] * cross, 0.0)
    before = last[pl.ds(jnp.maximum(column - 1, 0), 1), :]
    after = first[pl.ds(jnp.minimum(column + 1, COLS - 1), 1), :]
    rims_out[...] = two_rows(
        [
            jnp.where(column > 0, before, 0.0),
            jnp.where(column < COLS - 1, after, 0.0),
        ]
    )
    sums_out[...] = two_rows(sums)
    add_near_terms(meta, cols, pieces, (t0, t1, t2, t3), near)
    for m2, out in ((1, g1), (3, g3), (2, g2)):
        parts = far_group(meta, live, left, right, pieces, m2)
        encode(out, [part + near[4 * m2 + m] for m, part in enumerate(parts)], sums)


def adjoint_second_kernel(meta, live, left, right, a0, a1, a2, a3, b, near, own_out):
    pieces = data_pieces((a0, a1, a2, a3), b)
    for m, part in enumerate(far_group(meta, live, left, right, pieces, 0)):
        own_out[m * RHS : (m + 1) * RHS] = part + near[m]


def coefficient_pair(meta, live, right, held, s, slots):
    base_a, base_b = meta[M_ROW + s] * ROWS, meta[M_ROW + s + 1] * ROWS
    coef_a, coef_b = [], []
    for slot in slots:
        j = meta[slot]
        pair = jnp.concatenate([right[base_a + j], right[base_b + j]], axis=0)
        coef = (nt(held(slot), pair) * live_pair(live, base_a + j, base_b + j)).astype(BF16)
        coef_a.append(coef[:, :RANK])
        coef_b.append(coef[:, RANK:])
    return jnp.concatenate(coef_a, axis=1), jnp.concatenate(coef_b, axis=1)


def piece_of(arrays):
    def held(slot):
        return arrays[slot // 4][(slot % 4) * RHS : (slot % 4 + 1) * RHS]

    return held


def left_rows(meta, left, s, slots):
    base = meta[M_ROW + s] * ROWS
    return jnp.concatenate([left[base + meta[slot]] for slot in slots], axis=0)


def forward_near_kernel(meta, live, left, right, a, partial):
    for s in (4, 6, 0, 2):
        for at, coef in enumerate(coefficient_pair(meta, live, right, piece_of((a,)), s, range(4))):
            partial[s + at] = nn(coef, left_rows(meta, left, s + at, range(4)))


def forward_rows(meta, cols, live, left, right, partial, arrays, tiles, out, near, held, start):
    piece = piece_of(arrays)
    for slot in range(ROWS):
        held[slot] = piece(slot)
    for m in range(4):
        near[m] = partial[start + m]

    @pl.when(meta[M_OWNER] == 1)
    def _():
        for m in range(4):
            for k in range(BAND):
                slot = slot_of(meta, cols[start + m, k])
                near[m] += nt(held[slot], tile_at(tiles, start + m, k))

    for m in (0, 2):
        s = start + m
        for at, coef in enumerate(coefficient_pair(meta, live, right, piece, s, range(4, ROWS))):
            value = nn(coef, left_rows(meta, left, s + at, range(4, ROWS))) + near[m + at]
            out[(m + at) * RHS : (m + at + 1) * RHS] = value.astype(out.dtype)


def forward_first_kernel(
    meta, cols, live, left, right, partial, a, b1, b2, b3, t0, t1, t2, t3, out, held, near
):
    forward_rows(
        meta, cols, live, left, right, partial, (a, b1, b2, b3), (t0, t1, t2, t3), out, near, held, 4
    )


def forward_second_kernel(
    meta, cols, live, left, right, partial, a, b1, b2, b3, t0, t1, t2, t3, own, out, curved, edges, held, near
):
    forward_rows(
        meta, cols, live, left, right, partial, (a, b1, b2, b3), (t0, t1, t2, t3), out, near, held, 0
    )
    lane = lax.broadcasted_iota(jnp.int32, (RHS, LEAF), 1)
    for m in range(own.shape[0] // RHS):
        rows = slice(m * RHS, (m + 1) * RHS)
        vector, j = own[rows], meta[m]
        before = held[slot_of(meta, (j + ROWS - 1) % ROWS)][:, LEAF - RHS :].astype(F32)[:, RHS - 1 :]
        after = held[slot_of(meta, (j + 1) % ROWS)][:, :RHS].astype(F32)[:, :1]
        before = jnp.where(j == 0, 0.0, before)
        after = jnp.where(j == ROWS - 1, 0.0, after)
        below = jnp.where(lane == 0, before, pltpu.roll(vector, 1, 1))
        above = jnp.where(lane == LEAF - 1, after, pltpu.roll(vector, LEAF - 1, 1))
        curved[rows] = 2.0 * vector - below - above
    first = held[slot_of(meta, 0)][:, :RHS].astype(F32).T[:1]
    last = held[slot_of(meta, ROWS - 1)][:, LEAF - RHS :].astype(F32).T[RHS - 1 :]
    edges[...] = two_rows([first, last])


def without_rims(curved, before, after, j):
    lane = lax.broadcasted_iota(jnp.int32, (RHS, LEAF), 1)
    curved = curved - jnp.where((lane == 0) & (j == 0), before, 0.0)
    return curved - jnp.where((lane == LEAF - 1) & (j == ROWS - 1), after, 0.0)


def row_phase_first_kernel(own, g1, g3, g2, own_out, message):
    totals = [own[m * RHS : (m + 1) * RHS] for m in range(4)]
    for g in (g1, g3, g2):
        totals = [x + y for x, y in zip(totals, decode(g, 4))]
    zero = jnp.zeros((1, RHS), F32)
    encode(message, totals, [zero, zero])
    for m in range(4):
        own_out[m * RHS : (m + 1) * RHS] = totals[m]


def row_phase_kernel(own, sums_in, g1, g3, g2, own_out, sums_out, message):
    sums = [sums_in[0:1], sums_in[1:2]]
    totals = [own[m * RHS : (m + 1) * RHS] for m in range(4)]
    for g in (g1, g3, g2):
        sums = [x + y for x, y in zip(sums, decode_rows(g[4 * RHS :]))]
        totals = [x + y for x, y in zip(totals, decode(g, 4))]
    sums_out[...] = two_rows(sums)
    encode(message, totals, sums)
    for m in range(4):
        own_out[m * RHS : (m + 1) * RHS] = totals[m]


def group_totals(own, p1, p3, p2):
    totals = [own[m * RHS : (m + 1) * RHS] for m in range(4)]
    for k, p in ((1, p1), (3, p3), (2, p2)):
        got = decode(p, 4)
        totals = [total + got[k ^ m] for m, total in enumerate(totals)]
    return totals


def descent_kernel(own, p1, p3, p2, full, sent):
    for m, total in enumerate(group_totals(own, p1, p3, p2)):
        full[m * RHS : (m + 1) * RHS] = total
        sent[m * RHS : (m + 1) * RHS] = total.astype(BF16)


def descent2_kernel(meta, reg, first, curved, rims, own, sums_in, p1, p3, p2, full, sent, curved_out, sums_out):
    sums = [sums_in[0:1], sums_in[1:2]]
    for p in (p1, p3, p2):
        sums = [x + y for x, y in zip(sums, decode_rows(p[4 * RHS :]))]
    sums_out[...] = two_rows(sums)
    step, weight = as_column(sums[0] / sums[1]), as_column(reg[...])
    before, after = as_column(rims[0:1]), as_column(rims[1:2])
    for m, total in enumerate(group_totals(own, p1, p3, p2)):
        rows = slice(m * RHS, (m + 1) * RHS)
        whole = without_rims(curved[rows], before, after, meta[m])
        vector = first[rows] - step * (total + weight * whole)
        if m == 0:
            curved_out[...] = whole
            full[...] = vector
        sent[rows] = vector.astype(BF16)


def core_phase_kernel(own, other, own_out, p1, p3, p2):
    for m, out in ((1, p1), (3, p3), (2, p2), (0, own_out)):
        rows = slice(m * RHS, (m + 1) * RHS)
        out[...] = (own[rows] + other[rows].astype(F32)).astype(out.dtype)


def image_kernel(reg, vector, curved, edges, own, p1, p3, p2, full, message):
    total = own[...]
    for p in (p1, p3, p2):
        total += p[...].astype(F32)
    full[...] = total
    value = vector[:RHS]
    message[:RHS] = total.astype(BF16)
    gamma = row_sum(value * value)
    delta = row_sum(total * total) + reg[...] * row_sum(value * curved[:RHS])
    rows = jnp.concatenate(
        split3(gamma) + split3(delta) + [edges[0:2], jnp.zeros((EXTRA - 8, RHS), F32)], axis=0
    )
    message[RHS:] = jnp.concatenate([rows, jnp.zeros_like(rows)], axis=1).astype(BF16)


def image2_kernel(meta, reg, vector, curved, edges, curved_first, first, own, p1, p3, p2, full, sums):
    total = own[...]
    for p in (p1, p3, p2):
        total += p[...].astype(F32)
    full[...] = total
    value = vector[:RHS]
    weight = reg[...]
    sums[...] = jnp.zeros_like(sums)
    sums[0:1] = row_sum(value * value)
    sums[1:2] = row_sum(total * total) + weight * row_sum(value * curved[:RHS])
    sums[2:3] = row_sum(total * first[...]) + weight * row_sum(value * curved_first[:RHS])
    column = meta[M_COL]
    sums[pl.ds(8 + column, 1), :] = jnp.where(meta[M_AT] == 0, edges[0:1], 0.0)
    sums[pl.ds(16 + column, 1), :] = jnp.where(meta[M_AT] == 0, edges[1:2], 0.0)


def repeat_kernel(own, p1, p3, p2, out):
    total = own[...] + p1[...] + (p3[...] + p2[...])
    for k in range(ROWS):
        out[k * SUMS : (k + 1) * SUMS] = total


def transposed_kernel(*refs):
    sources, near, outs, (held, sems) = refs[:4], refs[4:6], refs[6:12], refs[12:]
    copies = [
        pltpu.make_async_copy(source.at[pl.ds(0, RHS)], held.at[k], sems.at[k]) for k, source in enumerate(sources)
    ]
    for copy in copies:
        copy.start()
    for value, out in zip(near, outs[4:]):
        out[...] = value[...].T
    for k, copy in enumerate(copies):
        copy.wait()
        outs[k][...] = held[k].T


def final_kernel(meta, reg, sums1, gathered, s1, s2, d1, d2, y1, y2, data, solution_out, misfit_out, curved_out, held):
    total = gathered[:SUMS]
    for k in range(1, ROWS):
        total += gathered[k * SUMS : (k + 1) * SUMS]
    held[...] = total
    gamma, delta = sums1[0:1], sums1[1:2]
    first, last = held[8 : 8 + COLS], held[16 : 16 + COLS]
    cross = jnp.sum(last[: COLS - 1] * first[1:], axis=0, keepdims=True)
    fresh, delta_new, delta_mixed = held[0:1], held[1:2] - 2.0 * reg[...] * cross, held[2:3]
    at, column = meta[M_AT], meta[M_COL]
    before = held[pl.ds(16 + jnp.maximum(column - 1, 0), 1), :]
    after = held[pl.ds(8 + jnp.minimum(column + 1, COLS - 1), 1), :]
    row = lax.broadcasted_iota(jnp.int32, (LEAF, RHS), 0)
    curved = d2[...] - jnp.where((row == 0) & (at == 0) & (column > 0), before, 0.0)
    curved -= jnp.where((row == LEAF - 1) & (at == ROWS - 1) & (column < COLS - 1), after, 0.0)
    beta = fresh / gamma
    delta2 = delta_new + 2.0 * beta * delta_mixed + beta * beta * delta
    two = fresh / delta2
    one = gamma / delta + two * beta
    solution_out[...] = one * s1[...] + two * s2[...]
    curved_out[...] = one * d1[...] + two * curved
    misfit_out[...] = data[...] - (one * y1[...] + two * y2[...])


def grid_pairs(move):
    return [(r * COLS + c, to) for r in range(ROWS) for c in range(COLS) for to in [move(r, c)] if to is not None]


def send(value, move):
    return lax.ppermute(value, ("row", "col"), grid_pairs(move))


def near_move(m):
    return lambda r, c: (r ^ (m if c % 2 == 0 else 4 * m)) * COLS + c


def far_move(m):
    return lambda r, c: (r ^ (4 * m if c % 2 == 0 else m)) * COLS + c


def y_move(m):
    return lambda r, c: r * COLS + (c ^ (2 * m))


def core_move(r, c):
    return r * COLS + (c ^ 1)


def tile_core_move(r, c):
    return r * COLS + (c ^ 1) if c % 2 != (r // 2) % 2 else None


def tile_move(m):
    def move(r, c):
        owner = r // 2
        there = c % 2 == owner % 2 and (c // 2) ^ (owner // 2) == m
        return r * COLS + (c ^ (2 * m)) if there else None

    return move


def per_device(far_left, far_right, far_rank, near_tiles, near_cols, data, reg_weight):
    r = lax.axis_index("row")
    c = lax.axis_index("col")
    odd = c % 2
    leaves = far_rank.shape[-1]

    def at_slot(m2, m1):
        return jnp.where(odd == 0, r ^ m1 ^ (4 * m2), r ^ (4 * m1) ^ m2)

    def slot_at(column):
        apart = column ^ r
        return jnp.where(odd == 1, (apart % 4) * 4 + apart // 4, apart)

    meta = jnp.stack(
        [at_slot(s // 4, s % 4) for s in range(ROWS)]
        + [c ^ (2 * (s % 4)) ^ (s // 4) for s in range(COLS)]
        + [slot_at((r + ROWS - 1) % ROWS), slot_at((r + 1) % ROWS)]
        + [(c == r // 2).astype(jnp.int32), r, odd, c]
    ).astype(jnp.int32)
    reg = reg_weight.reshape(1, RHS)
    data = data.reshape(LEAF, RHS)

    cols_row = jnp.pad(near_cols.astype(BF16), ((0, EXTRA - 1), (0, LEAF - BAND)))
    message = call(first_message, shape((MSG, LEAF), BF16), data, cols_row)

    def gather_col_pieces(mine):
        got = {m: send(mine, y_move(m)) for m in ORDER}
        return [mine, got[1], got[2], got[3]]

    group = gather_col_pieces(message)
    tiles = near_tiles.reshape(BAND, LEAF, LEAF)
    tiles = jnp.concatenate([tiles, send(tiles, tile_core_move)], axis=0)
    tiles = [tiles] + [send(tiles, tile_move(m)) for m in (1, 2, 3)]
    left = far_left.reshape(leaves, RANK, LEAF)
    right = far_right.reshape(leaves, RANK, LEAF)
    live = (lax.broadcasted_iota(jnp.int32, (leaves, RANK), 1) < far_rank.reshape(leaves, 1)).astype(F32)
    other = send(jnp.concatenate(group, axis=0), core_move)

    def factors():
        return [live] + [pltpu.with_memory_space_constraint(x, pltpu.VMEM) for x in (left, right)]

    vec, sums_shape = shape((RHS, LEAF)), shape((8, RHS))
    sent_shape = shape((RHS, LEAF), BF16)
    group4, group4_sent = shape((4 * RHS, LEAF)), shape((4 * RHS, LEAF), BF16)
    big = shape((4 * RHS + EXTRA, LEAF), jnp.int16)
    near_shape = shape((ROWS, RHS, LEAF))
    near_scratch = pltpu.VMEM((ROWS, RHS, LEAF), F32)

    def specs(scalars, vectors):
        return [SMEM] * scalars + [VMEM] * vectors

    def sum_over_row(own, sums, parts):
        got = [send(g, far_move(m)) for m, g in zip(ORDER, parts)]
        if sums is None:
            own, message = call(row_phase_first_kernel, (group4, big), own, *got)
        else:
            own, sums, message = call(row_phase_kernel, (group4, sums_shape, big), own, sums, *got)
        return own, sums, [send(message, near_move(m)) for m in ORDER]

    def product(vector, sent):
        got = {m: send(sent, far_move(m)) for m in ORDER}
        pieces = [sent, got[1], got[2], got[3]]
        partial = call(
            forward_near_kernel, shape((COLS, RHS, LEAF)), meta, *factors(), sent, specs=specs(1, 4), flops=1 << 29
        )
        scratch = [pltpu.VMEM((ROWS, RHS, LEAF), BF16), pltpu.VMEM((4, RHS, LEAF), F32)]
        parts = call(
            forward_first_kernel, group4_sent, meta, cols, *factors(), partial, *pieces, *tiles,
            specs=specs(2, 12), scratch=scratch, flops=1 << 30,
        )
        other = send(parts, core_move)
        own, curved, edges = call(
            forward_second_kernel, (group4, shape(vector.shape), sums_shape), meta, cols, *factors(), partial, *pieces, *tiles, vector,
            specs=specs(2, 13), scratch=scratch, flops=1 << 30,
        )
        own, p1, p3, p2 = call(core_phase_kernel, (vec, sent_shape, sent_shape, sent_shape), own, other)
        return curved, edges, [own] + [send(p, y_move(m)) for m, p in zip(ORDER, (p1, p3, p2))]

    far, cols = call(
        far_only_kernel, (near_shape, shape((COLS, RHS), jnp.int32)), meta, *factors(), *group, other,
        specs=specs(1, 8), flops=1 << 32,
    )
    g1, g3, g2, own = call(
        near_encode_kernel, (big, big, big, group4), meta, cols, far, *group, other, *tiles,
        specs=specs(2, 10), scratch=[near_scratch], flops=1 << 29,
    )
    own, _, parts = sum_over_row(own, None, (g1, g3, g2))
    s1, s1_sent = call(descent_kernel, (group4, group4_sent), own, *parts)
    d1, edges, parts = product(s1, s1_sent)
    y1, message = call(image_kernel, (vec, shape((MSG, LEAF), BF16)), reg, s1, d1, edges, *parts)

    group = gather_col_pieces(message)
    other = send(jnp.concatenate(group, axis=0), core_move)
    g1, g3, g2, near, sums, rims = call(
        adjoint_first_kernel, (big, big, big, near_shape, sums_shape, sums_shape),
        meta, cols, reg, *factors(), *group, other, *tiles,
        specs=specs(2, 13), scratch=[pltpu.VMEM((COLS, RHS), F32)] * 2, flops=1 << 30,
    )
    own = call(
        adjoint_second_kernel, group4, meta, *factors(), *group, other, near,
        specs=specs(1, 9), flops=1 << 30,
    )
    own, sums, parts = sum_over_row(own, sums, (g1, g3, g2))
    s2, s2_sent, d1, sums1 = call(
        descent2_kernel, (vec, group4_sent, vec, sums_shape), meta, reg, s1, d1, rims, own, sums, *parts,
        specs=specs(1, 9),
    )
    d2, edges, parts = product(s2, s2_sent)
    y2, sums2 = call(
        image2_kernel, (vec, shape((SUMS, RHS))), meta, reg, s2, d2, edges, d1, y1, *parts, specs=specs(1, 10)
    )
    sums2 = sums2 + send(sums2, core_move)
    got = [send(sums2, y_move(m)) for m in ORDER]
    repeated = call(repeat_kernel, shape((ROWS * SUMS, RHS)), sums2, *got)
    gathered = lax.all_to_all(repeated, "row", 0, 0, tiled=True)
    piece = shape((LEAF, RHS))
    in_hbm = [pltpu.with_memory_space_constraint(x, pltpu.HBM) for x in (s1, s2, d1, d2)]
    ready = call(
        transposed_kernel, (piece,) * 6, *in_hbm, y1, y2, specs=[HBM] * 4 + [VMEM] * 2,
        scratch=[pltpu.VMEM((4, RHS, LEAF), F32), pltpu.SemaphoreType.DMA((4,))],
    )
    solution_out, misfit_out, curved_out = call(
        final_kernel, (piece, piece, piece), meta, reg, sums1, gathered, *ready, data,
        specs=specs(1, 10), scratch=[pltpu.VMEM((SUMS, RHS), F32)],
    )
    whole = (1, 1, LEAF, RHS)
    return solution_out.reshape(whole), misfit_out.reshape(whole), curved_out.reshape(whole)


def solution(mesh):
    in_specs = (
        P("row", "col", None, None, None),
        P("row", "col", None, None, None),
        P("row", "col", None),
        P(("row", "col"), None, None, None),
        P(("row", "col"), None),
        P("row", "col", None, None),
        P(),
    )
    out_specs = (
        P("col", "row", None, None),
        P("row", "col", None, None),
        P("col", "row", None, None),
    )
    return jax.shard_map(
        per_device, mesh=mesh, in_specs=in_specs, out_specs=out_specs, check_vma=False
    )
```
